32 devices in a mesh: clip: 4 (over y, core), coarse: 4 (over z), fine: 2 (over x).
Axes of the slice: x: 2, y: 2, z: 4, core: 2. Of those that a mesh axis runs over, the one named last changes fastest.
Arguments:
- frames_in: bfloat16 [12, 1024, 1024], P('clip', ('coarse', 'fine')), may hold values from -6 to 6
- clip_lengths: int32 [12], P('clip'), may hold values from 512 to 1024, as said below
- out_grad: bfloat16 [12, 1024, 1024], P('clip', ('coarse', 'fine')), may hold values from -6 to 6
- first_up: float32 [1024, 4096], P('clip', ('coarse', 'fine')), may hold values from -0.1875 to 0.1875
- first_down: float32 [4096, 1024], P('clip', ('coarse', 'fine')), may hold values from -0.1875 to 0.1875
- query_weight: float32 [1024, 1024], P('clip', ('coarse', 'fine')), may hold values from -0.1875 to 0.1875
- key_weight: float32 [1024, 1024], P('clip', ('coarse', 'fine')), may hold values from -0.1875 to 0.1875
- value_weight: float32 [1024, 1024], P('clip', ('coarse', 'fine')), may hold values from -0.1875 to 0.1875
- output_weight: float32 [1024, 1024], P('clip', ('coarse', 'fine')), may hold values from -1.5 to 1.5
- pointwise_in: float32 [1024, 2048], P('clip', ('coarse', 'fine')), may hold values from -0.1875 to 0.1875
- pointwise_out: float32 [1024, 1024], P('clip', ('coarse', 'fine')), may hold values from -0.25 to 0.25
- second_up: float32 [1024, 4096], P('clip', ('coarse', 'fine')), may hold values from -0.1875 to 0.1875
- second_down: float32 [4096, 1024], P('clip', ('coarse', 'fine')), may hold values from -0.1875 to 0.1875
- norm_scales: float32 [6, 1024], replicated, may hold values from 0.25 to 1.75
- norm_shifts: float32 [6, 1024], replicated, may hold values from -1.75 to 1.75
- hidden_biases: float32 [2, 4096], replicated, may hold values from -3 to 3
- width_biases: float32 [4, 1024], replicated, may hold values from -1.75 to 1.75
- value_bias: float32 [1024], replicated, may hold values from -0.1875 to 0.1875
- relative_table: float32 [73, 64], replicated, may hold values from -6 to 6
- depth_kernel: float32 [31, 1024], replicated, may hold values from -1 to 1
Outputs:
- layer_out: bfloat16 [12, 1024, 1024], P('clip', ('coarse', 'fine'))
- in_grad: bfloat16 [12, 1024, 1024], P('clip', ('coarse', 'fine'))
- first_up_grad: float32 [1024, 4096], P('clip', ('coarse', 'fine'))
- first_down_grad: float32 [4096, 1024], P('clip', ('coarse', 'fine'))
- query_weight_grad: float32 [1024, 1024], P('clip', ('coarse', 'fine'))
- key_weight_grad: float32 [1024, 1024], P('clip', ('coarse', 'fine'))
- value_weight_grad: float32 [1024, 1024], P('clip', ('coarse', 'fine'))
- output_weight_grad: float32 [1024, 1024], P('clip', ('coarse', 'fine'))
- pointwise_in_grad: float32 [1024, 2048], P('clip', ('coarse', 'fine'))
- pointwise_out_grad: float32 [1024, 1024], P('clip', ('coarse', 'fine'))
- second_up_grad: float32 [1024, 4096], P('clip', ('coarse', 'fine'))
- second_down_grad: float32 [4096, 1024], P('clip', ('coarse', 'fine'))
- norm_scales_grad: float32 [6, 1024], replicated
- norm_shifts_grad: float32 [6, 1024], replicated
- hidden_biases_grad: float32 [2, 4096], replicated
- width_biases_grad: float32 [4, 1024], replicated
- value_bias_grad: float32 [1024], replicated
- relative_table_grad: float32 [73, 64], replicated
- depth_kernel_grad: float32 [31, 1024], replicated
The draws below stay inside these ranges and needn't reach their ends.
Inputs may be any that keep to these rules, and one draw needn't show every extreme that they name: `clip_lengths`: in each aligned block of 3 clips, at least one clip has all 1024 frames valid.
All inputs are finite; a program needn't handle non-finite values.
Results may differ from the reference program's by a relative error of at most 0.023.
Values may be sent and summed in bfloat16 or wider, within the bound.
No kernel may reach another device: no remote copies, remote signals or barrier semaphores. Data moves between devices by JAX's collectives and lax.ppermute only.
A program may use at most 320 MiB of HBM per device.

```python
import math
import jax
import jax.numpy as jnp
from jax import lax

D = 1024
HEADS = 16
HEAD_SIZE = 64
FF = 4096
KERNEL = 31
BACK_REACH = 64
FORE_REACH = 8
OFFSETS = 73
CLIP_LEN = 1024
CLIPS_DEV = 3
CLIPS = 12


def draw_clip_lengths(key, part):
    key = jax.random.fold_in(key, 11)
    first_key, second_key = jax.random.split(key)
    drawn = jax.random.randint(first_key, (CLIPS,), CLIP_LEN // 2, CLIP_LEN + 1)
    chosen = jax.random.randint(second_key, (CLIPS // CLIPS_DEV, 1), 0, CLIPS_DEV)
    full = (jnp.arange(CLIPS_DEV)[None, :] == chosen).reshape(CLIPS)
    return jnp.where(full, CLIP_LEN, drawn).astype(jnp.int32)


def block_levels(key, dims, shards, least, high):
    def one(position, parts):
        steps = jax.random.uniform(jax.random.fold_in(jax.random.fold_in(key, 6), position), (parts,), jnp.float32, least / len(shards), high / len(shards))
        return jnp.repeat(jnp.exp(steps), dims[position] // parts).reshape((-1,) + (1,) * (len(dims) - position - 1))

    loudness = one(*shards[0])
    for cut in shards[1:]:
        loudness = loudness * one(*cut)
    return loudness


def centred(own_key, dims, scale, most, cuts=(), held_as=jnp.bfloat16):
    values = scale * jax.random.normal(own_key, dims, jnp.float32)
    if cuts:
        values = values * block_levels(own_key, dims, cuts, -0.22, 0.18)
    return jnp.clip(values, -most, most).astype(held_as)


def setup_inputs(seed: int = 0) -> dict:
    key_of = jax.random.split(jax.random.key(seed), 21)
    frames_in = centred(key_of[0], (CLIPS, CLIP_LEN, D), 1.0, 6.0, ((0, 4), (1, 8)))
    clip_lengths = draw_clip_lengths(jax.random.fold_in(key_of[20], 71), 0)
    out_grad = centred(key_of[2], (CLIPS, CLIP_LEN, D), 1.0, 6.0, ((0, 4), (1, 8)))
    first_up = centred(key_of[3], (D, FF), D ** -0.5, 0.1875, ((0, 4), (1, 8)), jnp.float32)
    first_down = centred(key_of[4], (FF, D), (FF // 4) ** -0.5, 0.1875, ((0, 4), (1, 8)), jnp.float32)
    query_weight = centred(key_of[5], (D, D), D ** -0.5, 0.1875, ((0, 4), (1, 8)), jnp.float32)
    key_weight = centred(key_of[6], (D, D), D ** -0.5, 0.1875, ((0, 4), (1, 8)), jnp.float32)
    value_weight = centred(key_of[7], (D, D), D ** -0.5, 0.1875, ((0, 4), (1, 8)), jnp.float32)
    output_weight = centred(key_of[8], (D, D), (D * 16 // CLIP_LEN) ** -0.5, 1.5, ((0, 4), (1, 8)), jnp.float32)
    pointwise_in = centred(key_of[9], (D, 2 * D), D ** -0.5, 0.1875, ((0, 4), (1, 8)), jnp.float32)
    pointwise_out = centred(key_of[10], (D, D), (D // 2) ** -0.5, 0.25, ((0, 4), (1, 8)), jnp.float32)
    second_up = centred(key_of[11], (D, FF), D ** -0.5, 0.1875, ((0, 4), (1, 8)), jnp.float32)
    second_down = centred(key_of[12], (FF, D), (FF // 4) ** -0.5, 0.1875, ((0, 4), (1, 8)), jnp.float32)
    norm_scales = jnp.clip(1.0 + 0.15 * jax.random.normal(key_of[13], (6, D), jnp.float32), 0.25, 1.75)
    norm_shifts = centred(key_of[14], (6, D), 0.3, 1.75, (), jnp.float32)
    hidden_biases = centred(key_of[15], (2, FF), 0.5, 3.0, (), jnp.float32)
    width_biases = centred(key_of[16], (4, D), 0.3, 1.75, (), jnp.float32)
    value_bias = centred(key_of[17], (D,), 0.03, 0.1875, (), jnp.float32)
    relative_table = centred(key_of[18], (OFFSETS, HEAD_SIZE), 1.0, 6.0, (), jnp.float32)
    depth_kernel = centred(key_of[19], (KERNEL, D), KERNEL ** -0.5, 1.0, (), jnp.float32)
    return dict(frames_in=frames_in, clip_lengths=clip_lengths, out_grad=out_grad, first_up=first_up, first_down=first_down, query_weight=query_weight, key_weight=key_weight, value_weight=value_weight, output_weight=output_weight, pointwise_in=pointwise_in, pointwise_out=pointwise_out, second_up=second_up, second_down=second_down, norm_scales=norm_scales, norm_shifts=norm_shifts, hidden_biases=hidden_biases, width_biases=width_biases, value_bias=value_bias, relative_table=relative_table, depth_kernel=depth_kernel)


highest = lax.Precision.HIGHEST
negative_fill = -1e+30

@jax.custom_vjp
def low(v):
    return lax.optimization_barrier(v.astype(jnp.bfloat16)).astype(jnp.float32)

@jax.custom_vjp
def low_back(v):
    return v

def low_keep(v):
    return (low(v), None)

def low_pass(kept, grad):
    return (grad,)

def back_keep(v):
    return (v, None)

def back_low(kept, grad):
    return (low(grad),)
low.defvjp(low_keep, low_pass)
low_back.defvjp(back_keep, back_low)

def layer_norm(rows, scale, shift):
    middle = lax.optimization_barrier(jnp.mean(rows, -1, keepdims=True))
    centered = rows - middle
    spread = lax.optimization_barrier(jnp.mean(centered * centered, -1, keepdims=True))
    return centered * lax.rsqrt(spread + 1e-05) * scale + shift

def matmul_high(left, right):
    return jnp.matmul(left, right, precision=highest)

def glu_gate(doubled):
    half = doubled.shape[-1] // 2
    return doubled[..., :half] * jax.nn.sigmoid(doubled[..., half:])

def depthwise(extended, kernel):
    count = extended.shape[1] - kernel.shape[0] + 1
    return sum((kernel[tap] * extended[:, tap:tap + count] for tap in range(kernel.shape[0])))

def feed_forward(hidden, scale, shift, w_in, b_in, w_out, b_out):
    normed = low(layer_norm(hidden, scale, shift))
    upper = low_back(matmul_high(normed, w_in) + b_in)
    acted = low(jax.nn.silu(upper))
    return low_back(matmul_high(acted, w_out) + b_out)

def attention(hidden, lengths, scale, shift, w_query, b_query, w_key, w_value, b_value, w_output, b_output, table):
    group, length, width = hidden.shape
    normed = low(layer_norm(hidden, scale, shift))
    queries = low(low_back(matmul_high(normed, w_query) + b_query)).reshape(group, length, HEADS, HEAD_SIZE)
    key_heads = low(low_back(matmul_high(normed, w_key))).reshape(group, length, HEADS, HEAD_SIZE)
    value_heads = low(low_back(matmul_high(normed, w_value) + b_value)).reshape(group, length, HEADS, HEAD_SIZE)
    relative = low(low_back(jnp.einsum('glhd,rd->ghlr', queries, table, precision=highest)))
    positions = jnp.arange(length, dtype=jnp.int32)
    key_valid = positions[None, :] < lengths[:, None]

    def block_rows(index):
        first = index * 512
        query_block = lax.dynamic_slice_in_dim(queries, first, 512, 1)
        relative_block = lax.dynamic_slice_in_dim(relative, first, 512, 2)
        query_pos = first + jnp.arange(512, dtype=jnp.int32)
        offsets = jnp.clip(positions[None, :] - query_pos[:, None], -BACK_REACH, FORE_REACH) + BACK_REACH
        picked = jnp.take_along_axis(relative_block, jnp.broadcast_to(offsets, (group, HEADS, 512, length)), axis=3)
        dotted = jnp.einsum('gihd,gjhd->ghij', query_block, key_heads, precision=highest)
        scores = low_back((dotted + picked) * HEAD_SIZE ** (-0.5))
        scores = jnp.where(key_valid[:, None, None, :], scores, negative_fill)
        weights = low(jax.nn.softmax(scores, axis=-1))
        return jnp.einsum('ghij,gjhd->gihd', weights, value_heads, precision=highest)
    blocks = lax.map(jax.checkpoint(block_rows), jnp.arange(length // 512, dtype=jnp.int32))
    mixed = low(low_back(jnp.moveaxis(blocks, 0, 1).reshape(group, length, width)))
    return low_back(matmul_high(mixed, w_output) + b_output)

def convolve(hidden, lengths, scale, shift, w_in, kernel, scale_two, shift_two, w_out):
    length = hidden.shape[1]
    valid = (jnp.arange(length, dtype=jnp.int32)[None, :] < lengths[:, None])[:, :, None]
    normed = low(jnp.where(valid, layer_norm(hidden, scale, shift), 0.0))
    doubled = low_back(matmul_high(normed, w_in))
    gated = low(glu_gate(doubled))
    padded = jnp.pad(gated, ((0, 0), (KERNEL - 1, 0), (0, 0)))
    mixed = depthwise(padded, kernel)
    acted = low(jax.nn.silu(layer_norm(mixed, scale_two, shift_two)))
    return low_back(matmul_high(acted, w_out))

def layer(frames, lengths, params):
    first_up, first_down, query_weight, key_weight, value_weight, output_weight, pointwise_in, pointwise_out, second_up, second_down, norm_scales, norm_shifts, hidden_biases, width_biases, value_bias, relative_table, depth_kernel = params
    after_first = frames + 0.5 * feed_forward(frames, norm_scales[0], norm_shifts[0], low(first_up), hidden_biases[0], low(first_down), width_biases[0])
    after_attention = after_first + attention(after_first, lengths, norm_scales[1], norm_shifts[1], low(query_weight), width_biases[1], low(key_weight), low(value_weight), value_bias, low(output_weight), width_biases[2], low(relative_table))
    after_conv = after_attention + convolve(after_attention, lengths, norm_scales[2], norm_shifts[2], low(pointwise_in), depth_kernel, norm_scales[3], norm_shifts[3], low(pointwise_out))
    after_second = after_conv + 0.5 * feed_forward(after_conv, norm_scales[4], norm_shifts[4], low(second_up), hidden_biases[1], low(second_down), width_biases[3])
    return layer_norm(after_second, norm_scales[5], norm_shifts[5])

def reference(frames_in, clip_lengths, out_grad, first_up, first_down, query_weight, key_weight, value_weight, output_weight, pointwise_in, pointwise_out, second_up, second_down, norm_scales, norm_shifts, hidden_biases, width_biases, value_bias, relative_table, depth_kernel):
    params = (first_up, first_down, query_weight, key_weight, value_weight, output_weight, pointwise_in, pointwise_out, second_up, second_down, norm_scales, norm_shifts, hidden_biases, width_biases, value_bias, relative_table, depth_kernel)
    group = math.gcd(CLIPS, max(1, 4096 // CLIP_LEN))
    batches = CLIPS // group
    frames = frames_in.astype(jnp.float32).reshape(batches, group, CLIP_LEN, D)
    cotangent = out_grad.astype(jnp.float32).reshape(batches, group, CLIP_LEN, D)
    lengths = clip_lengths.reshape(batches, group)

    def step(totals, item):
        batch_frames, batch_lengths, batch_grad = item

        def forward(inputs, weights):
            return layer(inputs, batch_lengths, weights)
        result, pull = jax.vjp(forward, batch_frames, params)
        frame_grad, weight_grads = pull(batch_grad)
        return (jax.tree.map(jnp.add, totals, weight_grads), (result, frame_grad))
    totals, (results, frame_grads) = lax.scan(step, jax.tree.map(jnp.zeros_like, params), (frames, lengths, cotangent))
    return (results.reshape(CLIPS, CLIP_LEN, D).astype(jnp.bfloat16), frame_grads.reshape(CLIPS, CLIP_LEN, D).astype(jnp.bfloat16), totals[0], totals[1], totals[2], totals[3], totals[4], totals[5], totals[6], totals[7], totals[8], totals[9], totals[10], totals[11], totals[12], totals[13], totals[14], totals[15], totals[16])
```

```python
import functools

import jax
import jax.numpy as jnp
from jax import lax
from jax.experimental import pallas as pl
from jax.experimental.pallas import tpu as pltpu
from jax.sharding import PartitionSpec as P

D = 1024
HEADS = 16
HEAD_SIZE = 64
KERNEL = 31
BACK_REACH = 64
FORE_REACH = 8
OFFSETS = 73
TABLE_ROWS = 128
SEQ = ("coarse", "fine")
VMEM_BYTES = 56 * 1024 * 1024

negative_fill = -1e30
bf16 = jnp.bfloat16
f32 = jnp.float32


def log2(size):
    return size.bit_length() - 1


def swapped(shard, axis, bit):
    peers = lax.axis_size(axis)
    return lax.ppermute(shard, axis, [(i, i ^ (1 << bit)) for i in range(peers)])


def passed_along(shard, axis, by):
    peers = lax.axis_size(axis)
    pairs = [(i, i + by) for i in range(peers) if 0 <= i + by < peers]
    return lax.ppermute(shard, axis, pairs)


def layer_norm(rows, scale, shift):
    middle = jnp.mean(rows, -1, keepdims=True)
    centered = rows - middle
    spread = jnp.mean(centered * centered, -1, keepdims=True)
    return centered * lax.rsqrt(spread + 1e-05) * scale + shift


def norm_back(rows, scale, shift, grad):
    unused, pull = jax.vjp(layer_norm, rows, scale, shift)
    return pull(grad)


def glu_gate(doubled):
    half = doubled.shape[-1] // 2
    return doubled[..., :half] * jax.nn.sigmoid(doubled[..., half:])


def post_norm(mixed, scale, shift):
    return jax.nn.silu(layer_norm(mixed, scale, shift))


def depthwise(extended, kernel):
    count = extended.shape[1] - kernel.shape[0] + 1
    return sum((kernel[tap] * extended[:, tap : tap + count] for tap in range(kernel.shape[0])))


def product(left, right):
    return jnp.dot(left, right, preferred_element_type=f32)


def weight_grad(left, right):
    return lax.dot_general(left, right, (((0,), (0,)), ((), ())), preferred_element_type=f32)


def product_t(left, right):
    return lax.dot_general(left, right, (((1,), (1,)), ((), ())), preferred_element_type=f32)


def column_sum(values):
    return jnp.sum(values.astype(f32), 0)


def gather_steps(reverse):
    coarse = [("coarse", b) for b in range(log2(lax.axis_size("coarse")))]
    fine = [("fine", b) for b in range(log2(lax.axis_size("fine")))]
    upper = [("clip", b) for b in range(1, log2(lax.axis_size("clip")))]
    return coarse + (upper + fine if reverse else fine + upper)


def place_table(steps):
    count = 1 << len(steps)
    index = jnp.arange(count, dtype=jnp.int32)
    at = {
        axis: jnp.full((count,), lax.axis_index(axis), jnp.int32)
        for axis in ("clip", "coarse", "fine")
    }
    core = at["clip"] & 1
    for step, (axis, bit) in enumerate(steps):
        at[axis] = at[axis] ^ (((index >> step) & 1) << bit)
    column = at["coarse"] * lax.axis_size("fine") + at["fine"]
    return jnp.stack([column, at["clip"] >> 1, core])


def place_kernel(splits, table, own_ref, other_ref, *outs):
    width = own_ref.shape[2]
    core = table[2, 0]

    def write(first, second):
        start = 0
        for out, rows in zip(outs, splits):
            out[:, :width] = first[0, start : start + rows, :]
            out[:, width:] = second[0, start : start + rows, :]
            start += rows

    @pl.when(core == 0)
    def own_first():
        write(own_ref, other_ref)

    @pl.when(core != 0)
    def own_second():
        write(other_ref, own_ref)


def place(own, other, table, splits):
    pieces, rows, width = own.shape
    columns = lax.axis_size(SEQ)
    uppers = lax.axis_size("clip") // 2
    total = 2 * pieces * rows * width
    return pl.pallas_call(
        functools.partial(place_kernel, splits),
        out_shape=[
            jax.ShapeDtypeStruct((columns * part, uppers * 2 * width), bf16) for part in splits
        ],
        grid_spec=pltpu.PrefetchScalarGridSpec(
            num_scalar_prefetch=1,
            grid=(pieces,),
            in_specs=[
                pl.BlockSpec((1, rows, width), lambda p, table: (p, 0, 0)),
                pl.BlockSpec((1, rows, width), lambda p, table: (p, 0, 0)),
            ],
            out_specs=[
                pl.BlockSpec((part, 2 * width), lambda p, table: (table[0, p], table[1, p]))
                for part in splits
            ],
        ),
        compiler_params=pltpu.CompilerParams(vmem_limit_bytes=VMEM_BYTES),
        cost_estimate=pl.CostEstimate(flops=0, bytes_accessed=4 * total, transcendentals=0),
        name="place",
    )(table, own, other)


def gather_group(shard, steps):
    held = shard[None]
    for axis, bit in steps:
        held = jnp.concatenate([held, swapped(held, axis, bit)], 0)
    return held, swapped(held, "clip", 0)


def reduce_group(pairs, reverse):
    clip_count = lax.axis_size("clip")
    uppers = clip_count // 2
    sizes = {"coarse": lax.axis_size("coarse"), "fine": lax.axis_size("fine")}
    me = lax.axis_index("clip")
    width = pairs[0][0].shape[1] // clip_count
    parts = []
    for left, right in pairs:

        def blocks(core):
            return [
                lax.dynamic_slice_in_dim(left, (me ^ (2 * upper + core)) * width, width, 1)
                for upper in range(uppers)
            ]

        away = weight_grad(right, jnp.concatenate(blocks(1), 1)).astype(bf16)
        arrived = swapped(away, "clip", 0)
        kept = weight_grad(right, jnp.concatenate(blocks(0), 1)) + arrived.astype(f32)
        per_block = right.shape[1] // (sizes["coarse"] * sizes["fine"])
        parts.append(
            kept.astype(bf16).reshape(
                sizes["coarse"], sizes["fine"], per_block, uppers * width
            )
        )
    held = parts[0] if len(parts) == 1 else jnp.concatenate(parts, 2)
    coarse = [("coarse", b) for b in range(log2(sizes["coarse"]))][::-1]
    fine = [("fine", b) for b in range(log2(sizes["fine"]))][::-1]
    upper = [("clip", b) for b in range(1, log2(clip_count))][::-1]
    steps = (fine + upper if reverse else upper + fine) + coarse
    for count, (axis, bit) in enumerate(steps):
        if axis == "clip":
            half = held.shape[3] // 2
            away, kept = held[..., half:], held[..., :half]
        else:
            dim = 0 if axis == "coarse" else 1
            split = held.shape[:dim] + (2, held.shape[dim] // 2) + held.shape[dim + 1 :]
            mine = (lax.axis_index(axis) >> bit) & 1
            both = held.reshape(split)
            away = lax.dynamic_index_in_dim(both, 1 - mine, dim, keepdims=False)
            kept = lax.dynamic_index_in_dim(both, mine, dim, keepdims=False)
        total = kept.astype(f32) + swapped(away, axis, bit).astype(f32)
        held = total if count == len(steps) - 1 else total.astype(bf16)
    return held.reshape(held.shape[2], held.shape[3])


def summed_everywhere(values):
    for axis in ("clip", "fine", "coarse"):
        for bit in range(log2(lax.axis_size(axis))):
            values = values + swapped(values, axis, bit)
    return values


def packed(parts):
    flat = jnp.concatenate([part.reshape(-1) for part in parts])
    rows = -(-flat.shape[0] // 8192) * 8
    return jnp.pad(flat, (0, rows * D - flat.shape[0])).reshape(rows, D)


def unpacked(rows, parts):
    flat = rows.reshape(-1)
    out, start = [], 0
    for part in parts:
        out.append(flat[start : start + part.size].reshape(part.shape))
        start += part.size
    return out


def head_rows(ref, start, width):
    return ref[:, 0, :, start : start + width].reshape(-1, width)


def attend_kernel(lengths, x_ref, table_ref, out_ref, probs_ref):
    blocks, unused, block, wide = x_ref.shape
    length = blocks * block
    width = wide // 3
    valid = lengths[pl.program_id(0)]
    table = table_ref[...]
    key_at = lax.broadcasted_iota(jnp.int32, (1, length), 1)
    masked = key_at >= valid
    row_at = lax.broadcasted_iota(jnp.int32, (block, 3 * block), 0)
    offset = lax.broadcasted_iota(jnp.int32, (block, 3 * block), 1) - block - row_at
    for head in range(width // HEAD_SIZE):
        at = head * HEAD_SIZE
        keys = head_rows(x_ref, width + at, HEAD_SIZE)
        values = head_rows(x_ref, 2 * width + at, HEAD_SIZE)
        for part in range(blocks):
            queries = x_ref[part, 0, :, at : at + HEAD_SIZE]
            relative = product_t(queries, table).astype(bf16).astype(f32)
            back = relative[:, :1]
            fore = relative[:, OFFSETS - 1 : OFFSETS]
            band = jnp.concatenate([relative, jnp.zeros((block, 2 * block), f32)], 1)
            band = pltpu.roll(band, block - BACK_REACH, 1, stride=1, stride_axis=0)
            band = jnp.where(offset <= -BACK_REACH, back, jnp.where(offset >= FORE_REACH, fore, band))
            bias = []
            if part > 1:
                bias.append(jnp.broadcast_to(back, (block, (part - 1) * block)))
            bias.append(
                band[:, (block if part == 0 else 0) : (2 * block if part == blocks - 1 else 3 * block)]
            )
            if part < blocks - 2:
                bias.append(jnp.broadcast_to(fore, (block, (blocks - 2 - part) * block)))
            scores = (product_t(queries, keys) + jnp.concatenate(bias, 1)) * HEAD_SIZE ** (-0.5)
            scores = jnp.where(masked, negative_fill, scores)
            shifted = jnp.exp(scores - jnp.max(scores, -1, keepdims=True))
            probs = (shifted * (1.0 / jnp.sum(shifted, -1, keepdims=True))).astype(bf16)
            probs_ref[0, head, part * block : (part + 1) * block, :] = probs
            out_ref[part, 0, :, at : at + HEAD_SIZE] = product(probs, values).astype(bf16)


def attend_back_kernel(x_ref, grad_ref, probs_ref, table_ref, out_ref, table_out, score_g, relative_g):
    blocks, unused, block, wide = x_ref.shape
    width = wide // 3
    table = table_ref[...]
    scale = HEAD_SIZE ** (-0.5)
    row_at = lax.broadcasted_iota(jnp.int32, (block, 3 * block), 0)
    offset = lax.broadcasted_iota(jnp.int32, (block, 3 * block), 1) - block - row_at
    row_two = lax.broadcasted_iota(jnp.int32, (block, 2 * block), 0)
    lane = lax.broadcasted_iota(jnp.int32, (block, TABLE_ROWS), 1)
    zeros = jnp.zeros((block, block), f32)
    table_total = jnp.zeros(table_out.shape[1:], f32)
    for head in range(width // HEAD_SIZE):
        at = head * HEAD_SIZE
        all_queries = head_rows(x_ref, at, HEAD_SIZE)
        keys = head_rows(x_ref, width + at, HEAD_SIZE)
        values = head_rows(x_ref, 2 * width + at, HEAD_SIZE)
        all_grads = head_rows(grad_ref, at, HEAD_SIZE)
        for part in range(blocks):
            rows = slice(part * block, (part + 1) * block)
            grads = grad_ref[part, 0, :, at : at + HEAD_SIZE]
            probs = probs_ref[0, head, rows, :].astype(f32)
            probs_g = product_t(grads, values)
            inner = jnp.sum(probs * probs_g, -1, keepdims=True)
            low = (probs * (probs_g - inner)).astype(bf16)
            score_g[rows, :] = low
            wide_low = low.astype(f32)
            first = (part - 1) * block
            pieces = []
            if part == 0:
                pieces.append(zeros)
            pieces.append(wide_low[:, max(first, 0) : first + 3 * block])
            if part == blocks - 1:
                pieces.append(zeros)
            window = jnp.concatenate(pieces, 1)
            back = jnp.sum(jnp.where(offset <= -BACK_REACH, window, 0.0), -1, keepdims=True)
            fore = jnp.sum(jnp.where(offset >= FORE_REACH, window, 0.0), -1, keepdims=True)
            if part > 1:
                back = back + jnp.sum(wide_low[:, :first], -1, keepdims=True)
            if part < blocks - 2:
                fore = fore + jnp.sum(wide_low[:, first + 3 * block :], -1, keepdims=True)
            band = pltpu.roll(window, 3 * block - (block - BACK_REACH), 1)[:, : 2 * block]
            for bit in range(log2(block)):
                rolled = pltpu.roll(band, 2 * block - (1 << bit), 1)
                band = jnp.where(((row_two >> bit) & 1) == 1, rolled, band)
            band = band[:, :TABLE_ROWS]
            band = jnp.where(lane == 0, back, jnp.where(lane == OFFSETS - 1, fore, band))
            band = jnp.where(lane < OFFSETS, band, 0.0)
            relative = (band * scale).astype(bf16)
            relative_g[rows, :] = relative
            query_g = product(low, keys) * scale + product(relative, table)
            out_ref[part, 0, :, at : at + HEAD_SIZE] = query_g.astype(bf16)
        key_g = (weight_grad(score_g[...], all_queries) * scale).astype(bf16)
        value_g = weight_grad(probs_ref[0, head], all_grads).astype(bf16)
        table_total = table_total + weight_grad(relative_g[...], all_queries)
        for part in range(blocks):
            rows = slice(part * block, (part + 1) * block)
            out_ref[part, 0, :, width + at : width + at + HEAD_SIZE] = key_g[rows]
            out_ref[part, 0, :, 2 * width + at : 2 * width + at + HEAD_SIZE] = value_g[rows]
    table_out[0] = table_total


def attend(x, lengths, table):
    blocks, clips, block, wide = x.shape
    length, heads = blocks * block, wide // 3 // HEAD_SIZE
    return pl.pallas_call(
        attend_kernel,
        out_shape=[
            jax.ShapeDtypeStruct((blocks, clips, block, wide // 3), bf16),
            jax.ShapeDtypeStruct((clips, heads, length, length), bf16),
        ],
        grid_spec=pltpu.PrefetchScalarGridSpec(
            num_scalar_prefetch=1,
            grid=(clips,),
            in_specs=[
                pl.BlockSpec((blocks, 1, block, wide), lambda c, lengths: (0, c, 0, 0)),
                pl.BlockSpec((TABLE_ROWS, HEAD_SIZE), lambda c, lengths: (0, 0)),
            ],
            out_specs=[
                pl.BlockSpec((blocks, 1, block, wide // 3), lambda c, lengths: (0, c, 0, 0)),
                pl.BlockSpec((1, heads, length, length), lambda c, lengths: (c, 0, 0, 0)),
            ],
        ),
        compiler_params=pltpu.CompilerParams(vmem_limit_bytes=VMEM_BYTES),
        cost_estimate=pl.CostEstimate(
            flops=16 * clips * heads * length * length * HEAD_SIZE,
            bytes_accessed=2 * clips * heads * length * length,
            transcendentals=clips * heads * length * length,
        ),
        name="attend",
    )(lengths, x, table)


def attend_back(x, grads, probs, table):
    blocks, clips, block, wide = x.shape
    length, heads = blocks * block, wide // 3 // HEAD_SIZE
    return pl.pallas_call(
        attend_back_kernel,
        out_shape=[
            jax.ShapeDtypeStruct(x.shape, bf16),
            jax.ShapeDtypeStruct((clips, TABLE_ROWS, HEAD_SIZE), f32),
        ],
        grid=(clips,),
        in_specs=[
            pl.BlockSpec((blocks, 1, block, wide), lambda c: (0, c, 0, 0)),
            pl.BlockSpec((blocks, 1, block, wide // 3), lambda c: (0, c, 0, 0)),
            pl.BlockSpec((1, heads, length, length), lambda c: (c, 0, 0, 0)),
            pl.BlockSpec((TABLE_ROWS, HEAD_SIZE), lambda c: (0, 0)),
        ],
        out_specs=[
            pl.BlockSpec((blocks, 1, block, wide), lambda c: (0, c, 0, 0)),
            pl.BlockSpec((1, TABLE_ROWS, HEAD_SIZE), lambda c: (c, 0, 0)),
        ],
        scratch_shapes=[
            pltpu.VMEM((length, length), bf16),
            pltpu.VMEM((length, TABLE_ROWS), bf16),
        ],
        compiler_params=pltpu.CompilerParams(vmem_limit_bytes=VMEM_BYTES),
        cost_estimate=pl.CostEstimate(
            flops=32 * clips * heads * length * length * HEAD_SIZE,
            bytes_accessed=2 * clips * heads * length * length,
            transcendentals=0,
        ),
        name="attend_back",
    )(x, grads, probs, table)


def exchanged(rows):
    return lax.all_to_all(rows, SEQ, 0, 0, tiled=True)


class HeadsSplit:
    def __init__(self, clips, frames, lengths, table_low):
        self.clips, self.frames, self.lengths = clips, frames, lengths
        self.peers = lax.axis_size(SEQ)
        self.table = jnp.pad(table_low, ((0, TABLE_ROWS - OFFSETS), (0, 0)))

    def to_heads(self, rows):
        wide = rows.shape[1] // self.peers
        split = rows.reshape(self.clips * self.frames, self.peers, wide).transpose(1, 0, 2)
        return exchanged(split.reshape(self.peers, self.clips, self.frames, wide))

    def to_rows(self, blocks):
        wide = blocks.shape[3]
        back = exchanged(blocks).reshape(self.peers, self.clips * self.frames, wide)
        return back.transpose(1, 0, 2).reshape(self.clips * self.frames, self.peers * wide)

    def forward(self, rows):
        self.x = self.to_heads(rows)
        mixed, self.probs = attend(self.x, self.lengths, self.table)
        return self.to_rows(mixed)

    def backward(self, mixed_grad):
        grads, table_g = attend_back(self.x, self.to_heads(mixed_grad), self.probs, self.table)
        return self.to_rows(grads), jnp.sum(table_g, 0)[:OFFSETS]


class KeysGathered:
    def __init__(self, clips, frames, lengths, table_low):
        self.clips, self.frames, self.table = clips, frames, table_low
        self.peers = lax.axis_size(SEQ)
        length = frames * self.peers
        query_pos = lax.axis_index(SEQ) * frames + jnp.arange(frames, dtype=jnp.int32)
        key_pos = jnp.arange(length, dtype=jnp.int32)
        offset = jnp.clip(key_pos[None, :] - query_pos[:, None], -BACK_REACH, FORE_REACH)
        self.onehot = (
            (offset + BACK_REACH)[None] == jnp.arange(OFFSETS, dtype=jnp.int32)[:, None, None]
        ).astype(bf16)
        self.key_valid = key_pos[None, :] < lengths[:, None]

    def heads(self, rows):
        return rows.reshape(rows.shape[0], rows.shape[1], HEADS, HEAD_SIZE)

    def scores(self):
        dotted = jnp.einsum("cihd,cjhd->chij", self.queries, self.keys, preferred_element_type=f32)
        bias = jnp.einsum("chir,rij->chij", self.relative, self.onehot, preferred_element_type=f32)
        scaled = (dotted + bias) * HEAD_SIZE ** (-0.5)
        return jnp.where(self.key_valid[:, None, None, :], scaled, negative_fill)

    def forward(self, rows):
        split = rows.reshape(self.clips, self.frames, self.peers, 3, -1)
        flat = [split[:, :, :, which].reshape(self.clips, self.frames, D) for which in range(3)]
        self.queries = self.heads(flat[0])
        self.keys = self.heads(lax.all_gather(flat[1], SEQ, axis=1, tiled=True))
        self.values = self.heads(lax.all_gather(flat[2], SEQ, axis=1, tiled=True))
        self.relative = jnp.einsum(
            "cihd,rd->chir", self.queries, self.table, preferred_element_type=f32
        ).astype(bf16)
        scores = self.scores()
        top = jnp.max(scores, -1, keepdims=True)
        self.log_total = jnp.log(jnp.sum(jnp.exp(scores - top), -1, keepdims=True)) + top
        probs = jnp.exp(scores - self.log_total).astype(bf16)
        mixed = jnp.einsum("chij,cjhd->cihd", probs, self.values, preferred_element_type=f32)
        return mixed.astype(bf16).reshape(self.clips * self.frames, D)

    def backward(self, mixed_grad):
        scale = HEAD_SIZE ** (-0.5)
        grads = self.heads(mixed_grad.reshape(self.clips, self.frames, D))
        probs = jnp.exp(self.scores() - self.log_total)
        probs_g = jnp.einsum("cihd,cjhd->chij", grads, self.values, preferred_element_type=f32)
        inner = jnp.sum(probs * probs_g, -1, keepdims=True)
        scores_g = (probs * (probs_g - inner)).astype(bf16)
        relative_g = (
            jnp.einsum("chij,rij->chir", scores_g, self.onehot, preferred_element_type=f32) * scale
        ).astype(bf16)
        query_g = jnp.einsum(
            "chij,cjhd->cihd", scores_g, self.keys, preferred_element_type=f32
        ) * scale + jnp.einsum("chir,rd->cihd", relative_g, self.table, preferred_element_type=f32)
        table_g = jnp.einsum(
            "chir,cihd->rd", relative_g, self.queries, preferred_element_type=f32
        )
        key_g = (
            jnp.einsum("chij,cihd->cjhd", scores_g, self.queries, preferred_element_type=f32) * scale
        )
        value_g = jnp.einsum(
            "chij,cihd->cjhd", probs.astype(bf16), grads, preferred_element_type=f32
        )
        length = self.frames * self.peers
        both = [
            lax.psum_scatter(
                terms.reshape(self.clips, length, D).astype(bf16),
                SEQ,
                scatter_dimension=1,
                tiled=True,
            )
            for terms in (key_g, value_g)
        ]
        rows = self.clips * self.frames
        parts = [query_g.astype(bf16)] + both
        joined = jnp.stack([part.reshape(rows, self.peers, -1) for part in parts], 2)
        return joined.reshape(rows, 3 * D), table_g


def feed_forward(hidden, scale, shift, w_in, b_in, w_out, b_out):
    normed = layer_norm(hidden, scale, shift).astype(bf16)
    upper = product_t(normed, w_in) + b_in
    acted = jax.nn.silu(upper).astype(bf16)
    return (product_t(acted, w_out) + b_out, (normed, upper, acted))


def feed_back(grad, hidden, scale, shift, w_in, w_out, saved):
    normed, upper, acted = saved
    grad_low = grad.astype(bf16)
    unused, silu_pull = jax.vjp(jax.nn.silu, upper)
    upper_grad = silu_pull(product(grad_low, w_out))[0].astype(bf16)
    hidden_grad, scale_grad, shift_grad = norm_back(
        hidden, scale, shift, product(upper_grad, w_in)
    )
    return (
        hidden_grad,
        (normed, upper_grad),
        (acted, grad_low),
        scale_grad,
        shift_grad,
        column_sum(upper_grad),
        column_sum(grad_low),
    )


def per_device(
    frames_in,
    clip_lengths,
    out_grad,
    first_up,
    first_down,
    query_weight,
    key_weight,
    value_weight,
    output_weight,
    pointwise_in,
    pointwise_out,
    second_up,
    second_down,
    norm_scales,
    norm_shifts,
    hidden_biases,
    width_biases,
    value_bias,
    relative_table,
    depth_kernel,
):
    clips, frames, unused = frames_in.shape
    rows = clips * frames
    peers = lax.axis_size(SEQ)

    orders = [gather_steps(False), gather_steps(True)]
    tables = [place_table(steps) for steps in orders]
    groups = (
        ([first_up],),
        ([first_down],),
        ([query_weight, key_weight, value_weight], [output_weight]),
        ([pointwise_in], [pointwise_out]),
        ([second_up],),
        ([second_down],),
    )
    placed = []
    for number, group in enumerate(groups):
        shards = [shard.astype(bf16).T for part in group for shard in part]
        splits = tuple(sum(shard.shape[1] for shard in part) for part in group)
        order = number % 2
        own, other = gather_group(jnp.concatenate(shards, 0), orders[order])
        placed.extend(place(own, other, tables[order], splits))
    (
        up_first,
        down_first,
        inputs_full,
        output_full,
        inner_full,
        outer_full,
        up_second,
        down_second,
    ) = placed

    base = lax.axis_index(SEQ) * frames
    table_low = relative_table.astype(bf16)
    query_pos = base + jnp.arange(frames, dtype=jnp.int32)
    frame_valid = (query_pos[None, :] < clip_lengths[:, None]).reshape(rows, 1)
    share = D // peers
    inputs_bias = jnp.stack(
        [
            width_biases[1].reshape(peers, share),
            jnp.zeros((peers, share), f32),
            value_bias.reshape(peers, share),
        ],
        1,
    ).reshape(3 * D)

    start_rows = frames_in.astype(f32).reshape(rows, D)
    branch_one, first_saved = feed_forward(
        start_rows,
        norm_scales[0],
        norm_shifts[0],
        up_first,
        hidden_biases[0],
        down_first,
        width_biases[0],
    )
    after_first = start_rows + 0.5 * branch_one
    att_normed = layer_norm(after_first, norm_scales[1], norm_shifts[1]).astype(bf16)
    attention_rows = (product_t(att_normed, inputs_full) + inputs_bias).astype(bf16)
    split_heads = HEADS % peers == 0 and (D // peers) % 128 == 0
    attention = (HeadsSplit if split_heads else KeysGathered)(
        clips, frames, clip_lengths, table_low
    )
    mixed = attention.forward(attention_rows)
    after_attention = after_first + product_t(mixed, output_full) + width_biases[2]
    conv_normed = jnp.where(
        frame_valid, layer_norm(after_attention, norm_scales[2], norm_shifts[2]), 0.0
    ).astype(bf16)
    doubled = product_t(conv_normed, inner_full)
    gated = glu_gate(doubled).astype(bf16).reshape(clips, frames, D)
    carried = passed_along(gated[:, frames - KERNEL + 1 :], SEQ, 1)
    extended = jnp.concatenate([carried, gated], 1).astype(f32)
    mixed_conv = depthwise(extended, depth_kernel).reshape(rows, D)
    conv_acted = post_norm(mixed_conv, norm_scales[3], norm_shifts[3]).astype(bf16)
    after_conv = after_attention + product_t(conv_acted, outer_full)
    branch_two, second_saved = feed_forward(
        after_conv,
        norm_scales[4],
        norm_shifts[4],
        up_second,
        hidden_biases[1],
        down_second,
        width_biases[3],
    )
    after_second = after_conv + 0.5 * branch_two
    layer_out = (
        layer_norm(after_second, norm_scales[5], norm_shifts[5])
        .astype(bf16)
        .reshape(clips, frames, D)
    )

    final_grad, final_scale, final_shift = norm_back(
        after_second, norm_scales[5], norm_shifts[5], out_grad.astype(f32).reshape(rows, D)
    )
    (
        second_in,
        second_up_pair,
        second_down_pair,
        second_scale,
        second_shift,
        second_hidden,
        second_width,
    ) = feed_back(
        0.5 * final_grad,
        after_conv,
        norm_scales[4],
        norm_shifts[4],
        up_second,
        down_second,
        second_saved,
    )
    second_down_g = reduce_group([second_down_pair], False)
    second_up_g = reduce_group([second_up_pair], True)
    grad_conv = final_grad + second_in
    conv_low = grad_conv.astype(bf16)
    unused, post_pull = jax.vjp(post_norm, mixed_conv, norm_scales[3], norm_shifts[3])
    mixed_g, depth_scale, depth_shift = post_pull(product(conv_low, outer_full))
    unused, depth_pull = jax.vjp(depthwise, extended, depth_kernel)
    extended_g, kernel_g = depth_pull(mixed_g.reshape(clips, frames, D))
    returned = passed_along(extended_g[:, : KERNEL - 1].astype(bf16), SEQ, -1).astype(f32)
    own_g = extended_g[:, KERNEL - 1 :]
    gated_g = jnp.concatenate(
        [own_g[:, : frames - KERNEL + 1], own_g[:, frames - KERNEL + 1 :] + returned], 1
    ).reshape(rows, D)
    unused, glu_pull = jax.vjp(glu_gate, doubled)
    doubled_g = glu_pull(gated_g)[0].astype(bf16)
    normed_g = jnp.where(frame_valid, product(doubled_g, inner_full), 0.0)
    conv_in_g, conv_scale, conv_shift = norm_back(
        after_attention, norm_scales[2], norm_shifts[2], normed_g
    )
    grad_att = grad_conv + conv_in_g
    att_low = grad_att.astype(bf16)
    middle_g = reduce_group(
        [(conv_normed, doubled_g), (conv_acted, conv_low), (mixed, att_low)], False
    )
    mixed_grad = product(att_low, output_full).astype(bf16)
    attention_g, table_g = attention.backward(mixed_grad)
    inputs_g = reduce_group([(att_normed, attention_g)], True)
    att_in_g, att_scale, att_shift = norm_back(
        after_first, norm_scales[1], norm_shifts[1], product(attention_g, inputs_full)
    )
    grad_first = grad_att + att_in_g
    (
        first_in,
        first_up_pair,
        first_down_pair,
        first_scale,
        first_shift,
        first_hidden,
        first_width,
    ) = feed_back(
        0.5 * grad_first,
        start_rows,
        norm_scales[0],
        norm_shifts[0],
        up_first,
        down_first,
        first_saved,
    )
    first_down_g = reduce_group([first_down_pair], False)
    first_up_g = reduce_group([first_up_pair], True)
    in_grad = (grad_first + first_in).astype(bf16).reshape(clips, frames, D)

    attention_sums = column_sum(attention_g).reshape(peers, 3, share)
    early = [
        jnp.stack([att_scale, conv_scale, depth_scale, second_scale, final_scale]),
        jnp.stack([att_shift, conv_shift, depth_shift, second_shift, final_shift]),
        second_hidden[None],
        jnp.stack([attention_sums[:, 0].reshape(D), column_sum(att_low), second_width]),
        attention_sums[:, 2].reshape(D),
        table_g,
        kernel_g,
    ]
    late = [first_scale[None], first_shift[None], first_hidden[None], first_width[None]]
    early = unpacked(summed_everywhere(packed(early)), early)
    late = unpacked(summed_everywhere(packed(late)), late)

    inner_n = 2 * D // peers
    outer_n = D // peers
    return (
        layer_out,
        in_grad,
        first_up_g.T,
        first_down_g.T,
        inputs_g[:share].T,
        inputs_g[share : 2 * share].T,
        inputs_g[2 * share :].T,
        middle_g[inner_n + outer_n :].T,
        middle_g[:inner_n].T,
        middle_g[inner_n : inner_n + outer_n].T,
        second_up_g.T,
        second_down_g.T,
        jnp.concatenate([late[0], early[0]], 0),
        jnp.concatenate([late[1], early[1]], 0),
        jnp.concatenate([late[2], early[2]], 0),
        jnp.concatenate([late[3], early[3]], 0),
        early[4],
        early[5],
        early[6],
    )


def solution(mesh):
    block = P("clip", ("coarse", "fine"))
    rows = P("clip", ("coarse", "fine"), None)
    in_specs = (rows, P("clip"), rows) + (block,) * 10 + (P(),) * 7
    out_specs = (rows, rows) + (block,) * 10 + (P(),) * 7
    return jax.shard_map(
        per_device, mesh=mesh, in_specs=in_specs, out_specs=out_specs, check_vma=False
    )
```

```python
import functools

import jax
import jax.numpy as jnp
from jax import lax
from jax.experimental import pallas as pl
from jax.experimental.layout import Layout, with_layout_constraint
from jax.experimental.pallas import tpu as pltpu
from jax.sharding import PartitionSpec as P

D = 1024
HEADS = 16
HEAD_SIZE = 64
KERNEL = 31
BACK_REACH = 64
FORE_REACH = 8
OFFSETS = 73
TABLE_ROWS = 128
SEQ = ("coarse", "fine")
VMEM_BYTES = 56 * 1024 * 1024

negative_fill = -1e30
bf16 = jnp.bfloat16
f32 = jnp.float32


def log2(size):
    return size.bit_length() - 1


def swapped(shard, axis, bit):
    peers = lax.axis_size(axis)
    return lax.ppermute(shard, axis, [(i, i ^ (1 << bit)) for i in range(peers)])


def passed_along(shard, axis, by):
    peers = lax.axis_size(axis)
    pairs = [(i, i + by) for i in range(peers) if 0 <= i + by < peers]
    return lax.ppermute(shard, axis, pairs)


def layer_norm(rows, scale, shift):
    middle = jnp.mean(rows, -1, keepdims=True)
    centered = rows - middle
    spread = jnp.mean(centered * centered, -1, keepdims=True)
    return centered * lax.rsqrt(spread + 1e-05) * scale + shift


def norm_back(rows, scale, shift, grad):
    unused, pull = jax.vjp(layer_norm, rows, scale, shift)
    return pull(grad)


def glu_gate(doubled):
    half = doubled.shape[-1] // 2
    return doubled[..., :half] * jax.nn.sigmoid(doubled[..., half:])


def post_norm(mixed, scale, shift):
    return jax.nn.silu(layer_norm(mixed, scale, shift))


def depthwise(extended, kernel):
    count = extended.shape[1] - kernel.shape[0] + 1
    return sum((kernel[tap] * extended[:, tap : tap + count] for tap in range(kernel.shape[0])))


def product(left, right):
    return jnp.dot(left, right, preferred_element_type=f32)


def weight_grad(left, right):
    return lax.dot_general(left, right, (((0,), (0,)), ((), ())), preferred_element_type=f32)


def product_t(left, right):
    return lax.dot_general(left, right, (((1,), (1,)), ((), ())), preferred_element_type=f32)


def column_sum(values):
    return jnp.sum(values.astype(f32), 0)


def gather_steps(reverse):
    coarse = [("coarse", b) for b in range(log2(lax.axis_size("coarse")))]
    fine = [("fine", b) for b in range(log2(lax.axis_size("fine")))]
    upper = [("clip", b) for b in range(1, log2(lax.axis_size("clip")))]
    return coarse + (upper + fine if reverse else fine + upper)


def place_whole_kernel(splits, reverse, across, deep, uppers, here, own_ref, other_ref, *outs):
    width = own_ref.shape[-1]
    for left in range(across):
        for upper in range(uppers):
            for core, ref in enumerate((own_ref, other_ref)):
                piece = ref.at[left, upper, 0] if reverse else ref.at[upper, left, 0]
                lanes = pl.ds(
                    pl.multiple_of(((here[2] ^ upper) * 2 + (here[3] ^ core)) * width, 128), width
                )
                start = 0
                for out, rows in zip(outs, splits):
                    at = pl.multiple_of((here[1] ^ left) * rows, 16)
                    out[pl.ds(at, rows), lanes] = piece[start : start + rows, :]
                    start += rows


def place_whole(own, other, reverse, splits):
    pieces, rows, width = own.shape
    across, deep = lax.axis_size("fine"), lax.axis_size("coarse")
    uppers = lax.axis_size("clip") // 2
    lead = (across, uppers) if reverse else (uppers, across)
    me = lax.axis_index("clip")
    here = jnp.stack(
        [lax.axis_index("coarse"), lax.axis_index("fine"), me >> 1, me & 1]
    ).astype(jnp.int32)
    spec = pl.BlockSpec((*lead, 1, rows, width), lambda z, here: (0, 0, z, 0, 0))
    shape = (*lead, deep, rows, width)
    return pl.pallas_call(
        functools.partial(place_whole_kernel, splits, reverse, across, deep, uppers),
        out_shape=[
            jax.ShapeDtypeStruct((deep * across * part, uppers * 2 * width), bf16)
            for part in splits
        ],
        grid_spec=pltpu.PrefetchScalarGridSpec(
            num_scalar_prefetch=1,
            grid=(deep,),
            in_specs=[spec, spec],
            out_specs=[
                pl.BlockSpec(
                    (across * part, uppers * 2 * width), lambda z, here: (here[0] ^ z, 0)
                )
                for part in splits
            ],
        ),
        compiler_params=pltpu.CompilerParams(vmem_limit_bytes=VMEM_BYTES),
        cost_estimate=pl.CostEstimate(
            flops=0, bytes_accessed=8 * pieces * rows * width, transcendentals=0
        ),
        name="place",
    )(here, own.reshape(shape), other.reshape(shape))


def gather_group(shard, steps):
    held = with_layout_constraint(shard[None], Layout((0, 1, 2)))
    for axis, bit in steps:
        held = jnp.concatenate([held, swapped(held, axis, bit)], 0)
    return held, swapped(held, "clip", 0)


def reduce_group(pairs, reverse):
    clip_count = lax.axis_size("clip")
    uppers = clip_count // 2
    sizes = {"coarse": lax.axis_size("coarse"), "fine": lax.axis_size("fine")}
    me = lax.axis_index("clip")
    width = pairs[0][0].shape[1] // clip_count
    parts = []
    for left, right in pairs:

        def blocks(core):
            return [
                lax.dynamic_slice_in_dim(left, (me ^ (2 * upper + core)) * width, width, 1)
                for upper in range(uppers)
            ]

        away = weight_grad(right, jnp.concatenate(blocks(1), 1)).astype(bf16)
        arrived = swapped(away, "clip", 0)
        kept = weight_grad(right, jnp.concatenate(blocks(0), 1)) + arrived.astype(f32)
        per_block = right.shape[1] // (sizes["coarse"] * sizes["fine"])
        parts.append(
            kept.astype(bf16).reshape(
                sizes["coarse"], sizes["fine"], per_block, uppers * width
            )
        )
    held = parts[0] if len(parts) == 1 else jnp.concatenate(parts, 2)
    coarse = [("coarse", b) for b in range(log2(sizes["coarse"]))][::-1]
    fine = [("fine", b) for b in range(log2(sizes["fine"]))][::-1]
    upper = [("clip", b) for b in range(1, log2(clip_count))][::-1]
    steps = (fine + upper if reverse else upper + fine) + coarse
    for count, (axis, bit) in enumerate(steps):
        if axis == "clip":
            half = held.shape[3] // 2
            away, kept = held[..., half:], held[..., :half]
        else:
            dim = 0 if axis == "coarse" else 1
            split = held.shape[:dim] + (2, held.shape[dim] // 2) + held.shape[dim + 1 :]
            mine = (lax.axis_index(axis) >> bit) & 1
            both = held.reshape(split)
            away = lax.dynamic_index_in_dim(both, 1 - mine, dim, keepdims=False)
            kept = lax.dynamic_index_in_dim(both, mine, dim, keepdims=False)
        total = kept.astype(f32) + swapped(away, axis, bit).astype(f32)
        held = total if count == len(steps) - 1 else total.astype(bf16)
    return held.reshape(held.shape[2], held.shape[3])


def summed_everywhere(values):
    for axis in ("clip", "fine", "coarse"):
        for bit in range(log2(lax.axis_size(axis))):
            values = values + swapped(values, axis, bit)
    return values


def packed(parts):
    flat = jnp.concatenate([part.reshape(-1) for part in parts])
    rows = -(-flat.shape[0] // 8192) * 8
    return jnp.pad(flat, (0, rows * D - flat.shape[0])).reshape(rows, D)


def unpacked(rows, parts):
    flat = rows.reshape(-1)
    out, start = [], 0
    for part in parts:
        out.append(flat[start : start + part.size].reshape(part.shape))
        start += part.size
    return out


def head_rows(ref, start, width):
    return ref[:, 0, :, start : start + width].reshape(-1, width)


def attend_kernel(lengths, x_ref, table_ref, out_ref, probs_ref):
    blocks, unused, block, wide = x_ref.shape
    length = blocks * block
    width = wide // 3
    valid = lengths[pl.program_id(0)]
    table = table_ref[...]
    key_at = lax.broadcasted_iota(jnp.int32, (1, length), 1)
    masked = key_at >= valid
    row_at = lax.broadcasted_iota(jnp.int32, (block, 3 * block), 0)
    offset = lax.broadcasted_iota(jnp.int32, (block, 3 * block), 1) - block - row_at
    for head in range(width // HEAD_SIZE):
        at = head * HEAD_SIZE
        keys = head_rows(x_ref, width + at, HEAD_SIZE)
        values = head_rows(x_ref, 2 * width + at, HEAD_SIZE)
        for part in range(blocks):
            queries = x_ref[part, 0, :, at : at + HEAD_SIZE]
            relative = product_t(queries, table).astype(bf16).astype(f32)
            back = relative[:, :1]
            fore = relative[:, OFFSETS - 1 : OFFSETS]
            band = jnp.concatenate([relative, jnp.zeros((block, 2 * block), f32)], 1)
            band = pltpu.roll(band, block - BACK_REACH, 1, stride=1, stride_axis=0)
            band = jnp.where(offset <= -BACK_REACH, back, jnp.where(offset >= FORE_REACH, fore, band))
            bias = []
            if part > 1:
                bias.append(jnp.broadcast_to(back, (block, (part - 1) * block)))
            bias.append(
                band[:, (block if part == 0 else 0) : (2 * block if part == blocks - 1 else 3 * block)]
            )
            if part < blocks - 2:
                bias.append(jnp.broadcast_to(fore, (block, (blocks - 2 - part) * block)))
            scores = (product_t(queries, keys) + jnp.concatenate(bias, 1)) * HEAD_SIZE ** (-0.5)
            scores = jnp.where(masked, negative_fill, scores)
            shifted = jnp.exp(scores - jnp.max(scores, -1, keepdims=True))
            probs = (shifted * (1.0 / jnp.sum(shifted, -1, keepdims=True))).astype(bf16)
            probs_ref[0, head, part * block : (part + 1) * block, :] = probs
            out_ref[part, 0, :, at : at + HEAD_SIZE] = product(probs, values).astype(bf16)


def attend_back_kernel(x_ref, grad_ref, probs_ref, table_ref, out_ref, table_out, score_g, relative_g):
    blocks, unused, block, wide = x_ref.shape
    width = wide // 3
    table = table_ref[...]
    scale = HEAD_SIZE ** (-0.5)
    row_at = lax.broadcasted_iota(jnp.int32, (block, 3 * block), 0)
    offset = lax.broadcasted_iota(jnp.int32, (block, 3 * block), 1) - block - row_at
    row_two = lax.broadcasted_iota(jnp.int32, (block, 2 * block), 0)
    lane = lax.broadcasted_iota(jnp.int32, (block, TABLE_ROWS), 1)
    zeros = jnp.zeros((block, block), f32)
    table_total = jnp.zeros(table_out.shape[1:], f32)
    for head in range(width // HEAD_SIZE):
        at = head * HEAD_SIZE
        all_queries = head_rows(x_ref, at, HEAD_SIZE)
        keys = head_rows(x_ref, width + at, HEAD_SIZE)
        values = head_rows(x_ref, 2 * width + at, HEAD_SIZE)
        all_grads = head_rows(grad_ref, at, HEAD_SIZE)
        for part in range(blocks):
            rows = slice(part * block, (part + 1) * block)
            grads = grad_ref[part, 0, :, at : at + HEAD_SIZE]
            probs = probs_ref[0, head, rows, :].astype(f32)
            probs_g = product_t(grads, values)
            inner = jnp.sum(probs * probs_g, -1, keepdims=True)
            low = (probs * (probs_g - inner)).astype(bf16)
            score_g[rows, :] = low
            wide_low = low.astype(f32)
            first = (part - 1) * block
            pieces = []
            if part == 0:
                pieces.append(zeros)
            pieces.append(wide_low[:, max(first, 0) : first + 3 * block])
            if part == blocks - 1:
                pieces.append(zeros)
            window = jnp.concatenate(pieces, 1)
            back = jnp.sum(jnp.where(offset <= -BACK_REACH, window, 0.0), -1, keepdims=True)
            fore = jnp.sum(jnp.where(offset >= FORE_REACH, window, 0.0), -1, keepdims=True)
            if part > 1:
                back = back + jnp.sum(wide_low[:, :first], -1, keepdims=True)
            if part < blocks - 2:
                fore = fore + jnp.sum(wide_low[:, first + 3 * block :], -1, keepdims=True)
            band = pltpu.roll(window, 3 * block - (block - BACK_REACH), 1)[:, : 2 * block]
            for bit in range(log2(block)):
                rolled = pltpu.roll(band, 2 * block - (1 << bit), 1)
                band = jnp.where(((row_two >> bit) & 1) == 1, rolled, band)
            band = band[:, :TABLE_ROWS]
            band = jnp.where(lane == 0, back, jnp.where(lane == OFFSETS - 1, fore, band))
            band = jnp.where(lane < OFFSETS, band, 0.0)
            relative = (band * scale).astype(bf16)
            relative_g[rows, :] = relative
            query_g = product(low, keys) * scale + product(relative, table)
            out_ref[part, 0, :, at : at + HEAD_SIZE] = query_g.astype(bf16)
        key_g = (weight_grad(score_g[...], all_queries) * scale).astype(bf16)
        value_g = weight_grad(probs_ref[0, head], all_grads).astype(bf16)
        table_total = table_total + weight_grad(relative_g[...], all_queries)
        for part in range(blocks):
            rows = slice(part * block, (part + 1) * block)
            out_ref[part, 0, :, width + at : width + at + HEAD_SIZE] = key_g[rows]
            out_ref[part, 0, :, 2 * width + at : 2 * width + at + HEAD_SIZE] = value_g[rows]
    table_out[0] = table_total


def attend(x, lengths, table):
    blocks, clips, block, wide = x.shape
    length, heads = blocks * block, wide // 3 // HEAD_SIZE
    return pl.pallas_call(
        attend_kernel,
        out_shape=[
            jax.ShapeDtypeStruct((blocks, clips, block, wide // 3), bf16),
            jax.ShapeDtypeStruct((clips, heads, length, length), bf16),
        ],
        grid_spec=pltpu.PrefetchScalarGridSpec(
            num_scalar_prefetch=1,
            grid=(clips,),
            in_specs=[
                pl.BlockSpec((blocks, 1, block, wide), lambda c, lengths: (0, c, 0, 0)),
                pl.BlockSpec((TABLE_ROWS, HEAD_SIZE), lambda c, lengths: (0, 0)),
            ],
            out_specs=[
                pl.BlockSpec((blocks, 1, block, wide // 3), lambda c, lengths: (0, c, 0, 0)),
                pl.BlockSpec((1, heads, length, length), lambda c, lengths: (c, 0, 0, 0)),
            ],
        ),
        compiler_params=pltpu.CompilerParams(vmem_limit_bytes=VMEM_BYTES),
        cost_estimate=pl.CostEstimate(
            flops=16 * clips * heads * length * length * HEAD_SIZE,
            bytes_accessed=2 * clips * heads * length * length,
            transcendentals=clips * heads * length * length,
        ),
        name="attend",
    )(lengths, x, table)


def attend_back(x, grads, probs, table):
    blocks, clips, block, wide = x.shape
    length, heads = blocks * block, wide // 3 // HEAD_SIZE
    return pl.pallas_call(
        attend_back_kernel,
        out_shape=[
            jax.ShapeDtypeStruct(x.shape, bf16),
            jax.ShapeDtypeStruct((clips, TABLE_ROWS, HEAD_SIZE), f32),
        ],
        grid=(clips,),
        in_specs=[
            pl.BlockSpec((blocks, 1, block, wide), lambda c: (0, c, 0, 0)),
            pl.BlockSpec((blocks, 1, block, wide // 3), lambda c: (0, c, 0, 0)),
            pl.BlockSpec((1, heads, length, length), lambda c: (c, 0, 0, 0)),
            pl.BlockSpec((TABLE_ROWS, HEAD_SIZE), lambda c: (0, 0)),
        ],
        out_specs=[
            pl.BlockSpec((blocks, 1, block, wide), lambda c: (0, c, 0, 0)),
            pl.BlockSpec((1, TABLE_ROWS, HEAD_SIZE), lambda c: (c, 0, 0)),
        ],
        scratch_shapes=[
            pltpu.VMEM((length, length), bf16),
            pltpu.VMEM((length, TABLE_ROWS), bf16),
        ],
        compiler_params=pltpu.CompilerParams(vmem_limit_bytes=VMEM_BYTES),
        cost_estimate=pl.CostEstimate(
            flops=32 * clips * heads * length * length * HEAD_SIZE,
            bytes_accessed=2 * clips * heads * length * length,
            transcendentals=0,
        ),
        name="attend_back",
    )(x, grads, probs, table)


def exchanged(rows):
    return lax.all_to_all(rows, SEQ, 0, 0, tiled=True)


class HeadsSplit:
    def __init__(self, clips, frames, lengths, table_low):
        self.clips, self.frames, self.lengths = clips, frames, lengths
        self.peers = lax.axis_size(SEQ)
        self.table = jnp.pad(table_low, ((0, TABLE_ROWS - OFFSETS), (0, 0)))

    def to_heads(self, rows):
        wide = rows.shape[1] // self.peers
        split = rows.reshape(self.clips * self.frames, self.peers, wide).transpose(1, 0, 2)
        return exchanged(split.reshape(self.peers, self.clips, self.frames, wide))

    def to_rows(self, blocks):
        wide = blocks.shape[3]
        back = exchanged(blocks).reshape(self.peers, self.clips * self.frames, wide)
        return back.transpose(1, 0, 2).reshape(self.clips * self.frames, self.peers * wide)

    def forward(self, rows):
        self.x = self.to_heads(rows)
        mixed, self.probs = attend(self.x, self.lengths, self.table)
        return self.to_rows(mixed)

    def backward(self, mixed_grad):
        grads, table_g = attend_back(self.x, self.to_heads(mixed_grad), self.probs, self.table)
        return self.to_rows(grads), jnp.sum(table_g, 0)[:OFFSETS]


class KeysGathered:
    def __init__(self, clips, frames, lengths, table_low):
        self.clips, self.frames, self.table = clips, frames, table_low
        self.peers = lax.axis_size(SEQ)
        length = frames * self.peers
        query_pos = lax.axis_index(SEQ) * frames + jnp.arange(frames, dtype=jnp.int32)
        key_pos = jnp.arange(length, dtype=jnp.int32)
        offset = jnp.clip(key_pos[None, :] - query_pos[:, None], -BACK_REACH, FORE_REACH)
        self.onehot = (
            (offset + BACK_REACH)[None] == jnp.arange(OFFSETS, dtype=jnp.int32)[:, None, None]
        ).astype(bf16)
        self.key_valid = key_pos[None, :] < lengths[:, None]

    def heads(self, rows):
        return rows.reshape(rows.shape[0], rows.shape[1], HEADS, HEAD_SIZE)

    def scores(self):
        dotted = jnp.einsum("cihd,cjhd->chij", self.queries, self.keys, preferred_element_type=f32)
        bias = jnp.einsum("chir,rij->chij", self.relative, self.onehot, preferred_element_type=f32)
        scaled = (dotted + bias) * HEAD_SIZE ** (-0.5)
        return jnp.where(self.key_valid[:, None, None, :], scaled, negative_fill)

    def forward(self, rows):
        split = rows.reshape(self.clips, self.frames, self.peers, 3, -1)
        flat = [split[:, :, :, which].reshape(self.clips, self.frames, D) for which in range(3)]
        self.queries = self.heads(flat[0])
        self.keys = self.heads(lax.all_gather(flat[1], SEQ, axis=1, tiled=True))
        self.values = self.heads(lax.all_gather(flat[2], SEQ, axis=1, tiled=True))
        self.relative = jnp.einsum(
            "cihd,rd->chir", self.queries, self.table, preferred_element_type=f32
        ).astype(bf16)
        scores = self.scores()
        top = jnp.max(scores, -1, keepdims=True)
        self.log_total = jnp.log(jnp.sum(jnp.exp(scores - top), -1, keepdims=True)) + top
        probs = jnp.exp(scores - self.log_total).astype(bf16)
        mixed = jnp.einsum("chij,cjhd->cihd", probs, self.values, preferred_element_type=f32)
        return mixed.astype(bf16).reshape(self.clips * self.frames, D)

    def backward(self, mixed_grad):
        scale = HEAD_SIZE ** (-0.5)
        grads = self.heads(mixed_grad.reshape(self.clips, self.frames, D))
        probs = jnp.exp(self.scores() - self.log_total)
        probs_g = jnp.einsum("cihd,cjhd->chij", grads, self.values, preferred_element_type=f32)
        inner = jnp.sum(probs * probs_g, -1, keepdims=True)
        scores_g = (probs * (probs_g - inner)).astype(bf16)
        relative_g = (
            jnp.einsum("chij,rij->chir", scores_g, self.onehot, preferred_element_type=f32) * scale
        ).astype(bf16)
        query_g = jnp.einsum(
            "chij,cjhd->cihd", scores_g, self.keys, preferred_element_type=f32
        ) * scale + jnp.einsum("chir,rd->cihd", relative_g, self.table, preferred_element_type=f32)
        table_g = jnp.einsum(
            "chir,cihd->rd", relative_g, self.queries, preferred_element_type=f32
        )
        key_g = (
            jnp.einsum("chij,cihd->cjhd", scores_g, self.queries, preferred_element_type=f32) * scale
        )
        value_g = jnp.einsum(
            "chij,cihd->cjhd", probs.astype(bf16), grads, preferred_element_type=f32
        )
        length = self.frames * self.peers
        both = [
            lax.psum_scatter(
                terms.reshape(self.clips, length, D).astype(bf16),
                SEQ,
                scatter_dimension=1,
                tiled=True,
            )
            for terms in (key_g, value_g)
        ]
        rows = self.clips * self.frames
        parts = [query_g.astype(bf16)] + both
        joined = jnp.stack([part.reshape(rows, self.peers, -1) for part in parts], 2)
        return joined.reshape(rows, 3 * D), table_g


def feed_forward(hidden, scale, shift, w_in, b_in, w_out, b_out):
    normed = layer_norm(hidden, scale, shift).astype(bf16)
    upper = product_t(normed, w_in) + b_in
    acted = jax.nn.silu(upper).astype(bf16)
    return (product_t(acted, w_out) + b_out, (normed, upper, acted))


def feed_back(grad, hidden, scale, shift, w_in, w_out, saved):
    normed, upper, acted = saved
    grad_low = grad.astype(bf16)
    unused, silu_pull = jax.vjp(jax.nn.silu, upper)
    upper_grad = silu_pull(product(grad_low, w_out))[0].astype(bf16)
    hidden_grad, scale_grad, shift_grad = norm_back(
        hidden, scale, shift, product(upper_grad, w_in)
    )
    return (
        hidden_grad,
        (normed, upper_grad),
        (acted, grad_low),
        scale_grad,
        shift_grad,
        column_sum(upper_grad),
        column_sum(grad_low),
    )


def per_device(
    frames_in,
    clip_lengths,
    out_grad,
    first_up,
    first_down,
    query_weight,
    key_weight,
    value_weight,
    output_weight,
    pointwise_in,
    pointwise_out,
    second_up,
    second_down,
    norm_scales,
    norm_shifts,
    hidden_biases,
    width_biases,
    value_bias,
    relative_table,
    depth_kernel,
):
    clips, frames, unused = frames_in.shape
    rows = clips * frames
    peers = lax.axis_size(SEQ)

    orders = [gather_steps(False), gather_steps(True)]
    groups = (
        ([first_up],),
        ([first_down],),
        ([query_weight, key_weight, value_weight], [output_weight]),
        ([pointwise_in], [pointwise_out]),
        ([second_up],),
        ([second_down],),
    )
    placed = []
    for number, group in enumerate(groups):
        shards = [shard.astype(bf16).T for part in group for shard in part]
        splits = tuple(sum(shard.shape[1] for shard in part) for part in group)
        order = number % 2
        own, other = gather_group(jnp.concatenate(shards, 0), orders[order])
        placed.extend(place_whole(own, other, order == 1, splits))
    (
        up_first,
        down_first,
        inputs_full,
        output_full,
        inner_full,
        outer_full,
        up_second,
        down_second,
    ) = placed

    base = lax.axis_index(SEQ) * frames
    table_low = relative_table.astype(bf16)
    query_pos = base + jnp.arange(frames, dtype=jnp.int32)
    frame_valid = (query_pos[None, :] < clip_lengths[:, None]).reshape(rows, 1)
    share = D // peers
    inputs_bias = jnp.stack(
        [
            width_biases[1].reshape(peers, share),
            jnp.zeros((peers, share), f32),
            value_bias.reshape(peers, share),
        ],
        1,
    ).reshape(3 * D)

    start_rows = frames_in.astype(f32).reshape(rows, D)
    branch_one, first_saved = feed_forward(
        start_rows,
        norm_scales[0],
        norm_shifts[0],
        up_first,
        hidden_biases[0],
        down_first,
        width_biases[0],
    )
    after_first = start_rows + 0.5 * branch_one
    att_normed = layer_norm(after_first, norm_scales[1], norm_shifts[1]).astype(bf16)
    attention_rows = (product_t(att_normed, inputs_full) + inputs_bias).astype(bf16)
    split_heads = HEADS % peers == 0 and (D // peers) % 128 == 0
    attention = (HeadsSplit if split_heads else KeysGathered)(
        clips, frames, clip_lengths, table_low
    )
    mixed = attention.forward(attention_rows)
    after_attention = after_first + product_t(mixed, output_full) + width_biases[2]
    conv_normed = jnp.where(
        frame_valid, layer_norm(after_attention, norm_scales[2], norm_shifts[2]), 0.0
    ).astype(bf16)
    doubled = product_t(conv_normed, inner_full)
    gated = glu_gate(doubled).astype(bf16).reshape(clips, frames, D)
    carried = passed_along(gated[:, frames - KERNEL + 1 :], SEQ, 1)
    extended = jnp.concatenate([carried, gated], 1).astype(f32)
    mixed_conv = depthwise(extended, depth_kernel).reshape(rows, D)
    conv_acted = post_norm(mixed_conv, norm_scales[3], norm_shifts[3]).astype(bf16)
    after_conv = after_attention + product_t(conv_acted, outer_full)
    branch_two, second_saved = feed_forward(
        after_conv,
        norm_scales[4],
        norm_shifts[4],
        up_second,
        hidden_biases[1],
        down_second,
        width_biases[3],
    )
    after_second = after_conv + 0.5 * branch_two
    layer_out = (
        layer_norm(after_second, norm_scales[5], norm_shifts[5])
        .astype(bf16)
        .reshape(clips, frames, D)
    )

    final_grad, final_scale, final_shift = norm_back(
        after_second, norm_scales[5], norm_shifts[5], out_grad.astype(f32).reshape(rows, D)
    )
    (
        second_in,
        second_up_pair,
        second_down_pair,
        second_scale,
        second_shift,
        second_hidden,
        second_width,
    ) = feed_back(
        0.5 * final_grad,
        after_conv,
        norm_scales[4],
        norm_shifts[4],
        up_second,
        down_second,
        second_saved,
    )
    second_down_g = reduce_group([second_down_pair], False)
    second_up_g = reduce_group([second_up_pair], True)
    grad_conv = final_grad + second_in
    conv_low = grad_conv.astype(bf16)
    unused, post_pull = jax.vjp(post_norm, mixed_conv, norm_scales[3], norm_shifts[3])
    mixed_g, depth_scale, depth_shift = post_pull(product(conv_low, outer_full))
    unused, depth_pull = jax.vjp(depthwise, extended, depth_kernel)
    extended_g, kernel_g = depth_pull(mixed_g.reshape(clips, frames, D))
    returned = passed_along(extended_g[:, : KERNEL - 1].astype(bf16), SEQ, -1).astype(f32)
    own_g = extended_g[:, KERNEL - 1 :]
    gated_g = jnp.concatenate(
        [own_g[:, : frames - KERNEL + 1], own_g[:, frames - KERNEL + 1 :] + returned], 1
    ).reshape(rows, D)
    unused, glu_pull = jax.vjp(glu_gate, doubled)
    doubled_g = glu_pull(gated_g)[0].astype(bf16)
    normed_g = jnp.where(frame_valid, product(doubled_g, inner_full), 0.0)
    conv_in_g, conv_scale, conv_shift = norm_back(
        after_attention, norm_scales[2], norm_shifts[2], normed_g
    )
    grad_att = grad_conv + conv_in_g
    att_low = grad_att.astype(bf16)
    middle_g = reduce_group(
        [(conv_normed, doubled_g), (conv_acted, conv_low), (mixed, att_low)], False
    )
    mixed_grad = product(att_low, output_full).astype(bf16)
    attention_g, table_g = attention.backward(mixed_grad)
    inputs_g = reduce_group([(att_normed, attention_g)], True)
    att_in_g, att_scale, att_shift = norm_back(
        after_first, norm_scales[1], norm_shifts[1], product(attention_g, inputs_full)
    )
    grad_first = grad_att + att_in_g
    (
        first_in,
        first_up_pair,
        first_down_pair,
        first_scale,
        first_shift,
        first_hidden,
        first_width,
    ) = feed_back(
        0.5 * grad_first,
        start_rows,
        norm_scales[0],
        norm_shifts[0],
        up_first,
        down_first,
        first_saved,
    )
    first_down_g = reduce_group([first_down_pair], False)
    first_up_g = reduce_group([first_up_pair], True)
    in_grad = (grad_first + first_in).astype(bf16).reshape(clips, frames, D)

    attention_sums = column_sum(attention_g).reshape(peers, 3, share)
    early = [
        jnp.stack([att_scale, conv_scale, depth_scale, second_scale, final_scale]),
        jnp.stack([att_shift, conv_shift, depth_shift, second_shift, final_shift]),
        second_hidden[None],
        jnp.stack([attention_sums[:, 0].reshape(D), column_sum(att_low), second_width]),
        attention_sums[:, 2].reshape(D),
        table_g,
        kernel_g,
    ]
    late = [first_scale[None], first_shift[None], first_hidden[None], first_width[None]]
    early = unpacked(summed_everywhere(packed(early)), early)
    late = unpacked(summed_everywhere(packed(late)), late)

    inner_n = 2 * D // peers
    outer_n = D // peers
    return (
        layer_out,
        in_grad,
        first_up_g.T,
        first_down_g.T,
        inputs_g[:share].T,
        inputs_g[share : 2 * share].T,
        inputs_g[2 * share :].T,
        middle_g[inner_n + outer_n :].T,
        middle_g[:inner_n].T,
        middle_g[inner_n : inner_n + outer_n].T,
        second_up_g.T,
        second_down_g.T,
        jnp.concatenate([late[0], early[0]], 0),
        jnp.concatenate([late[1], early[1]], 0),
        jnp.concatenate([late[2], early[2]], 0),
        jnp.concatenate([late[3], early[3]], 0),
        early[4],
        early[5],
        early[6],
    )


def solution(mesh):
    block = P("clip", ("coarse", "fine"))
    rows = P("clip", ("coarse", "fine"), None)
    in_specs = (rows, P("clip"), rows) + (block,) * 10 + (P(),) * 7
    out_specs = (rows, rows) + (block,) * 10 + (P(),) * 7
    return jax.shard_map(
        per_device, mesh=mesh, in_specs=in_specs, out_specs=out_specs, check_vma=False
    )
```

```python
import functools

import jax
import jax.numpy as jnp
from jax import lax
from jax.experimental import pallas as pl
from jax.experimental.layout import Layout, with_layout_constraint
from jax.experimental.pallas import tpu as pltpu
from jax.sharding import PartitionSpec as P

D = 1024
HEADS = 16
HEAD_SIZE = 64
KERNEL = 31
BACK_REACH = 64
FORE_REACH = 8
OFFSETS = 73
TABLE_ROWS = 128
SEQ = ("coarse", "fine")
VMEM_BYTES = 56 * 1024 * 1024

negative_fill = -1e30
bf16 = jnp.bfloat16
f32 = jnp.float32


def log2(size):
    return size.bit_length() - 1


def swapped(shard, axis, bit):
    peers = lax.axis_size(axis)
    return lax.ppermute(shard, axis, [(i, i ^ (1 << bit)) for i in range(peers)])


def passed_along(shard, axis, by):
    peers = lax.axis_size(axis)
    pairs = [(i, i + by) for i in range(peers) if 0 <= i + by < peers]
    return lax.ppermute(shard, axis, pairs)


def layer_norm(rows, scale, shift):
    middle = jnp.mean(rows, -1, keepdims=True)
    centered = rows - middle
    spread = jnp.mean(centered * centered, -1, keepdims=True)
    return centered * lax.rsqrt(spread + 1e-05) * scale + shift


def norm_back(rows, scale, shift, grad):
    unused, pull = jax.vjp(layer_norm, rows, scale, shift)
    return pull(grad)


def glu_gate(doubled):
    half = doubled.shape[-1] // 2
    return doubled[..., :half] * jax.nn.sigmoid(doubled[..., half:])


def post_norm(mixed, scale, shift):
    return jax.nn.silu(layer_norm(mixed, scale, shift))


def depthwise(extended, kernel):
    count = extended.shape[1] - kernel.shape[0] + 1
    return sum((kernel[tap] * extended[:, tap : tap + count] for tap in range(kernel.shape[0])))


def product(left, right):
    return jnp.dot(left, right, preferred_element_type=f32)


def weight_grad(left, right):
    return lax.dot_general(left, right, (((0,), (0,)), ((), ())), preferred_element_type=f32)


def product_t(left, right):
    return lax.dot_general(left, right, (((1,), (1,)), ((), ())), preferred_element_type=f32)


def column_sum(values):
    return jnp.sum(values.astype(f32), 0)


def gather_steps(reverse):
    coarse = [("coarse", b) for b in range(log2(lax.axis_size("coarse")))]
    fine = [("fine", b) for b in range(log2(lax.axis_size("fine")))]
    upper = [("clip", b) for b in range(1, log2(lax.axis_size("clip")))]
    return coarse + (upper + fine if reverse else fine + upper)


def place_whole_kernel(splits, reverse, across, deep, uppers, here, own_ref, other_ref, *outs):
    width = own_ref.shape[-1]
    for left in range(across):
        for upper in range(uppers):
            for core, ref in enumerate((own_ref, other_ref)):
                piece = ref.at[left, upper, 0] if reverse else ref.at[upper, left, 0]
                lanes = pl.ds(
                    pl.multiple_of(((here[2] ^ upper) * 2 + (here[3] ^ core)) * width, 128), width
                )
                start = 0
                for out, rows in zip(outs, splits):
                    at = pl.multiple_of((here[1] ^ left) * rows, 16)
                    out[pl.ds(at, rows), lanes] = piece[start : start + rows, :]
                    start += rows


def place_whole(own, other, reverse, splits):
    pieces, rows, width = own.shape
    across, deep = lax.axis_size("fine"), lax.axis_size("coarse")
    uppers = lax.axis_size("clip") // 2
    lead = (across, uppers) if reverse else (uppers, across)
    me = lax.axis_index("clip")
    here = jnp.stack(
        [lax.axis_index("coarse"), lax.axis_index("fine"), me >> 1, me & 1]
    ).astype(jnp.int32)
    spec = pl.BlockSpec((*lead, 1, rows, width), lambda z, here: (0, 0, z, 0, 0))
    shape = (*lead, deep, rows, width)
    return pl.pallas_call(
        functools.partial(place_whole_kernel, splits, reverse, across, deep, uppers),
        out_shape=[
            jax.ShapeDtypeStruct((deep * across * part, uppers * 2 * width), bf16)
            for part in splits
        ],
        grid_spec=pltpu.PrefetchScalarGridSpec(
            num_scalar_prefetch=1,
            grid=(deep,),
            in_specs=[spec, spec],
            out_specs=[
                pl.BlockSpec(
                    (across * part, uppers * 2 * width), lambda z, here: (here[0] ^ z, 0)
                )
                for part in splits
            ],
        ),
        compiler_params=pltpu.CompilerParams(vmem_limit_bytes=VMEM_BYTES),
        cost_estimate=pl.CostEstimate(
            flops=0, bytes_accessed=8 * pieces * rows * width, transcendentals=0
        ),
        name="place",
    )(here, own.reshape(shape), other.reshape(shape))


def gather_group(shard, steps):
    held = with_layout_constraint(shard[None], Layout((0, 1, 2)))
    for axis, bit in steps:
        held = jnp.concatenate([held, swapped(held, axis, bit)], 0)
    return held, swapped(held, "clip", 0)


def reduce_group(pairs, reverse, begun=None):
    clip_count = lax.axis_size("clip")
    uppers = clip_count // 2
    sizes = {"coarse": lax.axis_size("coarse"), "fine": lax.axis_size("fine")}
    me = lax.axis_index("clip")
    width = pairs[0][0].shape[1] // clip_count
    parts = []
    for left, right in pairs:

        def blocks(core):
            return [
                lax.dynamic_slice_in_dim(left, (me ^ (2 * upper + core)) * width, width, 1)
                for upper in range(uppers)
            ]

        away = weight_grad(right, jnp.concatenate(blocks(1), 1)).astype(bf16)
        arrived = swapped(away, "clip", 0)
        kept = weight_grad(right, jnp.concatenate(blocks(0), 1)) + arrived.astype(f32)
        per_block = right.shape[1] // (sizes["coarse"] * sizes["fine"])
        parts.append(
            kept.astype(bf16).reshape(
                sizes["coarse"], sizes["fine"], per_block, uppers * width
            )
        )
    held = parts[0] if len(parts) == 1 else jnp.concatenate(parts, 2)
    if begun is not None:
        begun.append(held)
    coarse = [("coarse", b) for b in range(log2(sizes["coarse"]))][::-1]
    fine = [("fine", b) for b in range(log2(sizes["fine"]))][::-1]
    upper = [("clip", b) for b in range(1, log2(clip_count))][::-1]
    steps = (fine + upper if reverse else upper + fine) + coarse
    for count, (axis, bit) in enumerate(steps):
        if axis == "clip":
            half = held.shape[3] // 2
            away, kept = held[..., half:], held[..., :half]
        else:
            dim = 0 if axis == "coarse" else 1
            split = held.shape[:dim] + (2, held.shape[dim] // 2) + held.shape[dim + 1 :]
            mine = (lax.axis_index(axis) >> bit) & 1
            both = held.reshape(split)
            away = lax.dynamic_index_in_dim(both, 1 - mine, dim, keepdims=False)
            kept = lax.dynamic_index_in_dim(both, mine, dim, keepdims=False)
        total = kept.astype(f32) + swapped(away, axis, bit).astype(f32)
        held = total if count == len(steps) - 1 else total.astype(bf16)
    return held.reshape(held.shape[2], held.shape[3])


def summed_everywhere(values):
    for axis in ("coarse", "clip", "fine"):
        for bit in range(log2(lax.axis_size(axis))):
            values = values + swapped(values, axis, bit)
    return values


def packed(parts):
    flat = jnp.concatenate([part.reshape(-1) for part in parts])
    rows = -(-flat.shape[0] // 8192) * 8
    return jnp.pad(flat, (0, rows * D - flat.shape[0])).reshape(rows, D)


def unpacked(rows, parts):
    flat = rows.reshape(-1)
    out, start = [], 0
    for part in parts:
        out.append(flat[start : start + part.size].reshape(part.shape))
        start += part.size
    return out


def head_rows(ref, start, width):
    return ref[:, 0, :, start : start + width].reshape(-1, width)


def attend_kernel(lengths, x_ref, table_ref, out_ref, probs_ref):
    blocks, unused, block, wide = x_ref.shape
    length = blocks * block
    width = wide // 3
    valid = lengths[pl.program_id(0)]
    table = table_ref[...]
    key_at = lax.broadcasted_iota(jnp.int32, (1, length), 1)
    masked = key_at >= valid
    row_at = lax.broadcasted_iota(jnp.int32, (block, 3 * block), 0)
    offset = lax.broadcasted_iota(jnp.int32, (block, 3 * block), 1) - block - row_at
    for head in range(width // HEAD_SIZE):
        at = head * HEAD_SIZE
        keys = head_rows(x_ref, width + at, HEAD_SIZE)
        values = head_rows(x_ref, 2 * width + at, HEAD_SIZE)
        for part in range(blocks):
            queries = x_ref[part, 0, :, at : at + HEAD_SIZE]
            relative = product_t(queries, table).astype(bf16).astype(f32)
            back = relative[:, :1]
            fore = relative[:, OFFSETS - 1 : OFFSETS]
            band = jnp.concatenate([relative, jnp.zeros((block, 2 * block), f32)], 1)
            band = pltpu.roll(band, block - BACK_REACH, 1, stride=1, stride_axis=0)
            band = jnp.where(offset <= -BACK_REACH, back, jnp.where(offset >= FORE_REACH, fore, band))
            bias = []
            if part > 1:
                bias.append(jnp.broadcast_to(back, (block, (part - 1) * block)))
            bias.append(
                band[:, (block if part == 0 else 0) : (2 * block if part == blocks - 1 else 3 * block)]
            )
            if part < blocks - 2:
                bias.append(jnp.broadcast_to(fore, (block, (blocks - 2 - part) * block)))
            scores = (product_t(queries, keys) + jnp.concatenate(bias, 1)) * HEAD_SIZE ** (-0.5)
            scores = jnp.where(masked, negative_fill, scores)
            shifted = jnp.exp(scores - jnp.max(scores, -1, keepdims=True))
            probs = (shifted * (1.0 / jnp.sum(shifted, -1, keepdims=True))).astype(bf16)
            probs_ref[0, head, part * block : (part + 1) * block, :] = probs
            out_ref[part, 0, :, at : at + HEAD_SIZE] = product(probs, values).astype(bf16)


def attend_back_kernel(x_ref, grad_ref, probs_ref, table_ref, out_ref, table_out, score_g, relative_g):
    blocks, unused, block, wide = x_ref.shape
    width = wide // 3
    table = table_ref[...]
    scale = HEAD_SIZE ** (-0.5)
    row_at = lax.broadcasted_iota(jnp.int32, (block, 3 * block), 0)
    offset = lax.broadcasted_iota(jnp.int32, (block, 3 * block), 1) - block - row_at
    row_two = lax.broadcasted_iota(jnp.int32, (block, 2 * block), 0)
    lane = lax.broadcasted_iota(jnp.int32, (block, TABLE_ROWS), 1)
    zeros = jnp.zeros((block, block), f32)
    table_total = jnp.zeros(table_out.shape[1:], f32)
    for head in range(width // HEAD_SIZE):
        at = head * HEAD_SIZE
        all_queries = head_rows(x_ref, at, HEAD_SIZE)
        keys = head_rows(x_ref, width + at, HEAD_SIZE)
        values = head_rows(x_ref, 2 * width + at, HEAD_SIZE)
        all_grads = head_rows(grad_ref, at, HEAD_SIZE)
        for part in range(blocks):
            rows = slice(part * block, (part + 1) * block)
            grads = grad_ref[part, 0, :, at : at + HEAD_SIZE]
            probs = probs_ref[0, head, rows, :].astype(f32)
            probs_g = product_t(grads, values)
            inner = jnp.sum(probs * probs_g, -1, keepdims=True)
            low = (probs * (probs_g - inner)).astype(bf16)
            score_g[rows, :] = low
            wide_low = low.astype(f32)
            first = (part - 1) * block
            pieces = []
            if part == 0:
                pieces.append(zeros)
            pieces.append(wide_low[:, max(first, 0) : first + 3 * block])
            if part == blocks - 1:
                pieces.append(zeros)
            window = jnp.concatenate(pieces, 1)
            back = jnp.sum(jnp.where(offset <= -BACK_REACH, window, 0.0), -1, keepdims=True)
            fore = jnp.sum(jnp.where(offset >= FORE_REACH, window, 0.0), -1, keepdims=True)
            if part > 1:
                back = back + jnp.sum(wide_low[:, :first], -1, keepdims=True)
            if part < blocks - 2:
                fore = fore + jnp.sum(wide_low[:, first + 3 * block :], -1, keepdims=True)
            band = pltpu.roll(window, 3 * block - (block - BACK_REACH), 1)[:, : 2 * block]
            for bit in range(log2(block)):
                rolled = pltpu.roll(band, 2 * block - (1 << bit), 1)
                band = jnp.where(((row_two >> bit) & 1) == 1, rolled, band)
            band = band[:, :TABLE_ROWS]
            band = jnp.where(lane == 0, back, jnp.where(lane == OFFSETS - 1, fore, band))
            band = jnp.where(lane < OFFSETS, band, 0.0)
            relative = (band * scale).astype(bf16)
            relative_g[rows, :] = relative
            query_g = product(low, keys) * scale + product(relative, table)
            out_ref[part, 0, :, at : at + HEAD_SIZE] = query_g.astype(bf16)
        key_g = (weight_grad(score_g[...], all_queries) * scale).astype(bf16)
        value_g = weight_grad(probs_ref[0, head], all_grads).astype(bf16)
        table_total = table_total + weight_grad(relative_g[...], all_queries)
        for part in range(blocks):
            rows = slice(part * block, (part + 1) * block)
            out_ref[part, 0, :, width + at : width + at + HEAD_SIZE] = key_g[rows]
            out_ref[part, 0, :, 2 * width + at : 2 * width + at + HEAD_SIZE] = value_g[rows]
    table_out[0] = table_total


def attend(x, lengths, table):
    blocks, clips, block, wide = x.shape
    length, heads = blocks * block, wide // 3 // HEAD_SIZE
    return pl.pallas_call(
        attend_kernel,
        out_shape=[
            jax.ShapeDtypeStruct((blocks, clips, block, wide // 3), bf16),
            jax.ShapeDtypeStruct((clips, heads, length, length), bf16),
        ],
        grid_spec=pltpu.PrefetchScalarGridSpec(
            num_scalar_prefetch=1,
            grid=(clips,),
            in_specs=[
                pl.BlockSpec((blocks, 1, block, wide), lambda c, lengths: (0, c, 0, 0)),
                pl.BlockSpec((TABLE_ROWS, HEAD_SIZE), lambda c, lengths: (0, 0)),
            ],
            out_specs=[
                pl.BlockSpec((blocks, 1, block, wide // 3), lambda c, lengths: (0, c, 0, 0)),
                pl.BlockSpec((1, heads, length, length), lambda c, lengths: (c, 0, 0, 0)),
            ],
        ),
        compiler_params=pltpu.CompilerParams(vmem_limit_bytes=VMEM_BYTES),
        cost_estimate=pl.CostEstimate(
            flops=16 * clips * heads * length * length * HEAD_SIZE,
            bytes_accessed=2 * clips * heads * length * length,
            transcendentals=clips * heads * length * length,
        ),
        name="attend",
    )(lengths, x, table)


def attend_back(x, grads, probs, table):
    blocks, clips, block, wide = x.shape
    length, heads = blocks * block, wide // 3 // HEAD_SIZE
    return pl.pallas_call(
        attend_back_kernel,
        out_shape=[
            jax.ShapeDtypeStruct(x.shape, bf16),
            jax.ShapeDtypeStruct((clips, TABLE_ROWS, HEAD_SIZE), f32),
        ],
        grid=(clips,),
        in_specs=[
            pl.BlockSpec((blocks, 1, block, wide), lambda c: (0, c, 0, 0)),
            pl.BlockSpec((blocks, 1, block, wide // 3), lambda c: (0, c, 0, 0)),
            pl.BlockSpec((1, heads, length, length), lambda c: (c, 0, 0, 0)),
            pl.BlockSpec((TABLE_ROWS, HEAD_SIZE), lambda c: (0, 0)),
        ],
        out_specs=[
            pl.BlockSpec((blocks, 1, block, wide), lambda c: (0, c, 0, 0)),
            pl.BlockSpec((1, TABLE_ROWS, HEAD_SIZE), lambda c: (c, 0, 0)),
        ],
        scratch_shapes=[
            pltpu.VMEM((length, length), bf16),
            pltpu.VMEM((length, TABLE_ROWS), bf16),
        ],
        compiler_params=pltpu.CompilerParams(vmem_limit_bytes=VMEM_BYTES),
        cost_estimate=pl.CostEstimate(
            flops=32 * clips * heads * length * length * HEAD_SIZE,
            bytes_accessed=2 * clips * heads * length * length,
            transcendentals=0,
        ),
        name="attend_back",
    )(x, grads, probs, table)


def exchanged(rows):
    return lax.all_to_all(rows, SEQ, 0, 0, tiled=True)


class HeadsSplit:
    def __init__(self, clips, frames, lengths, table_low):
        self.clips, self.frames, self.lengths = clips, frames, lengths
        self.peers = lax.axis_size(SEQ)
        self.table = jnp.pad(table_low, ((0, TABLE_ROWS - OFFSETS), (0, 0)))

    def to_heads(self, rows):
        wide = rows.shape[1] // self.peers
        split = rows.reshape(self.clips * self.frames, self.peers, wide).transpose(1, 0, 2)
        return exchanged(split.reshape(self.peers, self.clips, self.frames, wide))

    def to_rows(self, blocks):
        wide = blocks.shape[3]
        back = exchanged(blocks).reshape(self.peers, self.clips * self.frames, wide)
        return back.transpose(1, 0, 2).reshape(self.clips * self.frames, self.peers * wide)

    def forward(self, rows):
        self.x = self.to_heads(rows)
        mixed, self.probs = attend(self.x, self.lengths, self.table)
        return self.to_rows(mixed)

    def backward(self, mixed_grad):
        grads, table_g = attend_back(self.x, self.to_heads(mixed_grad), self.probs, self.table)
        return self.to_rows(grads), jnp.sum(table_g, 0)[:OFFSETS]


class KeysGathered:
    def __init__(self, clips, frames, lengths, table_low):
        self.clips, self.frames, self.table = clips, frames, table_low
        self.peers = lax.axis_size(SEQ)
        length = frames * self.peers
        query_pos = lax.axis_index(SEQ) * frames + jnp.arange(frames, dtype=jnp.int32)
        key_pos = jnp.arange(length, dtype=jnp.int32)
        offset = jnp.clip(key_pos[None, :] - query_pos[:, None], -BACK_REACH, FORE_REACH)
        self.onehot = (
            (offset + BACK_REACH)[None] == jnp.arange(OFFSETS, dtype=jnp.int32)[:, None, None]
        ).astype(bf16)
        self.key_valid = key_pos[None, :] < lengths[:, None]

    def heads(self, rows):
        return rows.reshape(rows.shape[0], rows.shape[1], HEADS, HEAD_SIZE)

    def scores(self):
        dotted = jnp.einsum("cihd,cjhd->chij", self.queries, self.keys, preferred_element_type=f32)
        bias = jnp.einsum("chir,rij->chij", self.relative, self.onehot, preferred_element_type=f32)
        scaled = (dotted + bias) * HEAD_SIZE ** (-0.5)
        return jnp.where(self.key_valid[:, None, None, :], scaled, negative_fill)

    def forward(self, rows):
        split = rows.reshape(self.clips, self.frames, self.peers, 3, -1)
        flat = [split[:, :, :, which].reshape(self.clips, self.frames, D) for which in range(3)]
        self.queries = self.heads(flat[0])
        self.keys = self.heads(lax.all_gather(flat[1], SEQ, axis=1, tiled=True))
        self.values = self.heads(lax.all_gather(flat[2], SEQ, axis=1, tiled=True))
        self.relative = jnp.einsum(
            "cihd,rd->chir", self.queries, self.table, preferred_element_type=f32
        ).astype(bf16)
        scores = self.scores()
        top = jnp.max(scores, -1, keepdims=True)
        self.log_total = jnp.log(jnp.sum(jnp.exp(scores - top), -1, keepdims=True)) + top
        probs = jnp.exp(scores - self.log_total).astype(bf16)
        mixed = jnp.einsum("chij,cjhd->cihd", probs, self.values, preferred_element_type=f32)
        return mixed.astype(bf16).reshape(self.clips * self.frames, D)

    def backward(self, mixed_grad):
        scale = HEAD_SIZE ** (-0.5)
        grads = self.heads(mixed_grad.reshape(self.clips, self.frames, D))
        probs = jnp.exp(self.scores() - self.log_total)
        probs_g = jnp.einsum("cihd,cjhd->chij", grads, self.values, preferred_element_type=f32)
        inner = jnp.sum(probs * probs_g, -1, keepdims=True)
        scores_g = (probs * (probs_g - inner)).astype(bf16)
        relative_g = (
            jnp.einsum("chij,rij->chir", scores_g, self.onehot, preferred_element_type=f32) * scale
        ).astype(bf16)
        query_g = jnp.einsum(
            "chij,cjhd->cihd", scores_g, self.keys, preferred_element_type=f32
        ) * scale + jnp.einsum("chir,rd->cihd", relative_g, self.table, preferred_element_type=f32)
        table_g = jnp.einsum(
            "chir,cihd->rd", relative_g, self.queries, preferred_element_type=f32
        )
        key_g = (
            jnp.einsum("chij,cihd->cjhd", scores_g, self.queries, preferred_element_type=f32) * scale
        )
        value_g = jnp.einsum(
            "chij,cihd->cjhd", probs.astype(bf16), grads, preferred_element_type=f32
        )
        length = self.frames * self.peers
        both = [
            lax.psum_scatter(
                terms.reshape(self.clips, length, D).astype(bf16),
                SEQ,
                scatter_dimension=1,
                tiled=True,
            )
            for terms in (key_g, value_g)
        ]
        rows = self.clips * self.frames
        parts = [query_g.astype(bf16)] + both
        joined = jnp.stack([part.reshape(rows, self.peers, -1) for part in parts], 2)
        return joined.reshape(rows, 3 * D), table_g


def feed_forward(hidden, scale, shift, w_in, b_in, w_out, b_out):
    normed = layer_norm(hidden, scale, shift).astype(bf16)
    upper = product_t(normed, w_in) + b_in
    acted = jax.nn.silu(upper).astype(bf16)
    return (product_t(acted, w_out) + b_out, (normed, upper, acted))


def feed_back(grad, hidden, scale, shift, w_in, w_out, saved):
    normed, upper, acted = saved
    grad_low = grad.astype(bf16)
    unused, silu_pull = jax.vjp(jax.nn.silu, upper)
    upper_grad = silu_pull(product(grad_low, w_out))[0].astype(bf16)
    hidden_grad, scale_grad, shift_grad = norm_back(
        hidden, scale, shift, product(upper_grad, w_in)
    )
    return (
        hidden_grad,
        (normed, upper_grad),
        (acted, grad_low),
        scale_grad,
        shift_grad,
        column_sum(upper_grad),
        column_sum(grad_low),
    )


def per_device(
    frames_in,
    clip_lengths,
    out_grad,
    first_up,
    first_down,
    query_weight,
    key_weight,
    value_weight,
    output_weight,
    pointwise_in,
    pointwise_out,
    second_up,
    second_down,
    norm_scales,
    norm_shifts,
    hidden_biases,
    width_biases,
    value_bias,
    relative_table,
    depth_kernel,
):
    clips, frames, unused = frames_in.shape
    rows = clips * frames
    peers = lax.axis_size(SEQ)

    orders = [gather_steps(False), gather_steps(True)]
    groups = (
        ([first_up],),
        ([first_down],),
        ([query_weight, key_weight, value_weight], [output_weight]),
        ([pointwise_in], [pointwise_out]),
        ([second_up],),
        ([second_down],),
    )
    placed = []
    for number, group in enumerate(groups):
        shards = [shard.astype(bf16).T for part in group for shard in part]
        splits = tuple(sum(shard.shape[1] for shard in part) for part in group)
        order = number % 2
        own, other = gather_group(jnp.concatenate(shards, 0), orders[order])
        placed.extend(place_whole(own, other, order == 1, splits))
    (
        up_first,
        down_first,
        inputs_full,
        output_full,
        inner_full,
        outer_full,
        up_second,
        down_second,
    ) = placed

    base = lax.axis_index(SEQ) * frames
    table_low = relative_table.astype(bf16)
    query_pos = base + jnp.arange(frames, dtype=jnp.int32)
    frame_valid = (query_pos[None, :] < clip_lengths[:, None]).reshape(rows, 1)
    share = D // peers
    inputs_bias = jnp.stack(
        [
            width_biases[1].reshape(peers, share),
            jnp.zeros((peers, share), f32),
            value_bias.reshape(peers, share),
        ],
        1,
    ).reshape(3 * D)

    start_rows = frames_in.astype(f32).reshape(rows, D)
    branch_one, first_saved = feed_forward(
        start_rows,
        norm_scales[0],
        norm_shifts[0],
        up_first,
        hidden_biases[0],
        down_first,
        width_biases[0],
    )
    after_first = start_rows + 0.5 * branch_one
    att_normed = layer_norm(after_first, norm_scales[1], norm_shifts[1]).astype(bf16)
    attention_rows = (product_t(att_normed, inputs_full) + inputs_bias).astype(bf16)
    split_heads = HEADS % peers == 0 and (D // peers) % 128 == 0
    attention = (HeadsSplit if split_heads else KeysGathered)(
        clips, frames, clip_lengths, table_low
    )
    mixed = attention.forward(attention_rows)
    after_attention = after_first + product_t(mixed, output_full) + width_biases[2]
    conv_normed = jnp.where(
        frame_valid, layer_norm(after_attention, norm_scales[2], norm_shifts[2]), 0.0
    ).astype(bf16)
    doubled = product_t(conv_normed, inner_full)
    gated = glu_gate(doubled).astype(bf16).reshape(clips, frames, D)
    carried = passed_along(gated[:, frames - KERNEL + 1 :], SEQ, 1)
    extended = jnp.concatenate([carried, gated], 1).astype(f32)
    mixed_conv = depthwise(extended, depth_kernel).reshape(rows, D)
    conv_acted = post_norm(mixed_conv, norm_scales[3], norm_shifts[3]).astype(bf16)
    after_conv = after_attention + product_t(conv_acted, outer_full)
    branch_two, second_saved = feed_forward(
        after_conv,
        norm_scales[4],
        norm_shifts[4],
        up_second,
        hidden_biases[1],
        down_second,
        width_biases[3],
    )
    after_second = after_conv + 0.5 * branch_two
    layer_out = (
        layer_norm(after_second, norm_scales[5], norm_shifts[5])
        .astype(bf16)
        .reshape(clips, frames, D)
    )

    final_grad, final_scale, final_shift = norm_back(
        after_second, norm_scales[5], norm_shifts[5], out_grad.astype(f32).reshape(rows, D)
    )
    (
        second_in,
        second_up_pair,
        second_down_pair,
        second_scale,
        second_shift,
        second_hidden,
        second_width,
    ) = feed_back(
        0.5 * final_grad,
        after_conv,
        norm_scales[4],
        norm_shifts[4],
        up_second,
        down_second,
        second_saved,
    )
    second_down_g = reduce_group([second_down_pair], False)
    second_up_g = reduce_group([second_up_pair], True)
    grad_conv = final_grad + second_in
    conv_low = grad_conv.astype(bf16)
    unused, post_pull = jax.vjp(post_norm, mixed_conv, norm_scales[3], norm_shifts[3])
    mixed_g, depth_scale, depth_shift = post_pull(product(conv_low, outer_full))
    unused, depth_pull = jax.vjp(depthwise, extended, depth_kernel)
    extended_g, kernel_g = depth_pull(mixed_g.reshape(clips, frames, D))
    returned = passed_along(extended_g[:, : KERNEL - 1].astype(bf16), SEQ, -1).astype(f32)
    own_g = extended_g[:, KERNEL - 1 :]
    gated_g = jnp.concatenate(
        [own_g[:, : frames - KERNEL + 1], own_g[:, frames - KERNEL + 1 :] + returned], 1
    ).reshape(rows, D)
    unused, glu_pull = jax.vjp(glu_gate, doubled)
    doubled_g = glu_pull(gated_g)[0].astype(bf16)
    normed_g = jnp.where(frame_valid, product(doubled_g, inner_full), 0.0)
    conv_in_g, conv_scale, conv_shift = norm_back(
        after_attention, norm_scales[2], norm_shifts[2], normed_g
    )
    grad_att = grad_conv + conv_in_g
    att_low = grad_att.astype(bf16)
    middle_g = reduce_group(
        [(conv_normed, doubled_g), (conv_acted, conv_low), (mixed, att_low)], False
    )
    mixed_grad = product(att_low, output_full).astype(bf16)
    attention_g, table_g = attention.backward(mixed_grad)
    begun = []
    inputs_g = reduce_group([(att_normed, attention_g)], True, begun)
    att_in_g, att_scale, att_shift = norm_back(
        after_first, norm_scales[1], norm_shifts[1], product(attention_g, inputs_full)
    )
    grad_first = grad_att + att_in_g
    (
        first_in,
        first_up_pair,
        first_down_pair,
        first_scale,
        first_shift,
        first_hidden,
        first_width,
    ) = feed_back(
        0.5 * grad_first,
        start_rows,
        norm_scales[0],
        norm_shifts[0],
        up_first,
        down_first,
        first_saved,
    )
    first_down_g = reduce_group([first_down_pair], False, begun)
    first_up_g = reduce_group([first_up_pair], True, begun)
    in_grad = (grad_first + first_in).astype(bf16).reshape(clips, frames, D)

    attention_sums = column_sum(attention_g).reshape(peers, 3, share)
    small = [
        jnp.stack([first_scale, att_scale, conv_scale, depth_scale, second_scale, final_scale]),
        jnp.stack([first_shift, att_shift, conv_shift, depth_shift, second_shift, final_shift]),
        jnp.stack([first_hidden, second_hidden]),
        jnp.stack(
            [first_width, attention_sums[:, 0].reshape(D), column_sum(att_low), second_width]
        ),
        attention_sums[:, 2].reshape(D),
        table_g,
        kernel_g,
    ]
    values, unused = lax.optimization_barrier((packed(small), begun))
    small = unpacked(summed_everywhere(values), small)

    inner_n = 2 * D // peers
    outer_n = D // peers
    return (
        layer_out,
        in_grad,
        first_up_g.T,
        first_down_g.T,
        inputs_g[:share].T,
        inputs_g[share : 2 * share].T,
        inputs_g[2 * share :].T,
        middle_g[inner_n + outer_n :].T,
        middle_g[:inner_n].T,
        middle_g[inner_n : inner_n + outer_n].T,
        second_up_g.T,
        second_down_g.T,
        *small,
    )


def solution(mesh):
    block = P("clip", ("coarse", "fine"))
    rows = P("clip", ("coarse", "fine"), None)
    in_specs = (rows, P("clip"), rows) + (block,) * 10 + (P(),) * 7
    out_specs = (rows, rows) + (block,) * 10 + (P(),) * 7
    return jax.shard_map(
        per_device, mesh=mesh, in_specs=in_specs, out_specs=out_specs, check_vma=False
    )
```

```python
import functools

import jax
import jax.numpy as jnp
from jax import lax
from jax.experimental import pallas as pl
from jax.experimental.layout import Layout, with_layout_constraint
from jax.experimental.pallas import tpu as pltpu
from jax.sharding import PartitionSpec as P

D = 1024
HEADS = 16
HEAD_SIZE = 64
KERNEL = 31
BACK_REACH = 64
FORE_REACH = 8
OFFSETS = 73
TABLE_ROWS = 128
SEQ = ("coarse", "fine")
VMEM_BYTES = 56 * 1024 * 1024

negative_fill = -1e30
bf16 = jnp.bfloat16
f32 = jnp.float32


def log2(size):
    return size.bit_length() - 1


def swapped(shard, axis, bit):
    peers = lax.axis_size(axis)
    return lax.ppermute(shard, axis, [(i, i ^ (1 << bit)) for i in range(peers)])


def passed_along(shard, axis, by):
    peers = lax.axis_size(axis)
    pairs = [(i, i + by) for i in range(peers) if 0 <= i + by < peers]
    return lax.ppermute(shard, axis, pairs)


def layer_norm(rows, scale, shift):
    middle = jnp.mean(rows, -1, keepdims=True)
    centered = rows - middle
    spread = jnp.mean(centered * centered, -1, keepdims=True)
    return centered * lax.rsqrt(spread + 1e-05) * scale + shift


def norm_back(rows, scale, shift, grad):
    unused, pull = jax.vjp(layer_norm, rows, scale, shift)
    return pull(grad)


def glu_gate(doubled):
    half = doubled.shape[-1] // 2
    return doubled[..., :half] * jax.nn.sigmoid(doubled[..., half:])


def post_norm(mixed, scale, shift):
    return jax.nn.silu(layer_norm(mixed, scale, shift))


def depthwise(extended, kernel):
    count = extended.shape[1] - kernel.shape[0] + 1
    return sum((kernel[tap] * extended[:, tap : tap + count] for tap in range(kernel.shape[0])))


def product(left, right):
    return jnp.dot(left, right, preferred_element_type=f32)


def weight_grad(left, right):
    return lax.dot_general(left, right, (((0,), (0,)), ((), ())), preferred_element_type=f32)


def product_t(left, right):
    return lax.dot_general(left, right, (((1,), (1,)), ((), ())), preferred_element_type=f32)


def column_sum(values):
    return jnp.sum(values.astype(f32), 0)


def gather_steps(reverse):
    coarse = [("coarse", b) for b in range(log2(lax.axis_size("coarse")))]
    fine = [("fine", b) for b in range(log2(lax.axis_size("fine")))]
    upper = [("clip", b) for b in range(1, log2(lax.axis_size("clip")))]
    return coarse + (upper + fine if reverse else fine + upper)


def place_whole_kernel(splits, reverse, across, deep, uppers, here, own_ref, other_ref, *outs):
    width = own_ref.shape[-1]
    for left in range(across):
        for upper in range(uppers):
            for core, ref in enumerate((own_ref, other_ref)):
                piece = ref.at[left, upper, 0] if reverse else ref.at[upper, left, 0]
                lanes = pl.ds(
                    pl.multiple_of(((here[2] ^ upper) * 2 + (here[3] ^ core)) * width, 128), width
                )
                start = 0
                for out, rows in zip(outs, splits):
                    at = pl.multiple_of((here[1] ^ left) * rows, 16)
                    out[pl.ds(at, rows), lanes] = piece[start : start + rows, :]
                    start += rows


def place_whole(own, other, reverse, splits):
    pieces, rows, width = own.shape
    across, deep = lax.axis_size("fine"), lax.axis_size("coarse")
    uppers = lax.axis_size("clip") // 2
    lead = (across, uppers) if reverse else (uppers, across)
    me = lax.axis_index("clip")
    here = jnp.stack(
        [lax.axis_index("coarse"), lax.axis_index("fine"), me >> 1, me & 1]
    ).astype(jnp.int32)
    spec = pl.BlockSpec((*lead, 1, rows, width), lambda z, here: (0, 0, z, 0, 0))
    shape = (*lead, deep, rows, width)
    return pl.pallas_call(
        functools.partial(place_whole_kernel, splits, reverse, across, deep, uppers),
        out_shape=[
            jax.ShapeDtypeStruct((deep * across * part, uppers * 2 * width), bf16)
            for part in splits
        ],
        grid_spec=pltpu.PrefetchScalarGridSpec(
            num_scalar_prefetch=1,
            grid=(deep,),
            in_specs=[spec, spec],
            out_specs=[
                pl.BlockSpec(
                    (across * part, uppers * 2 * width), lambda z, here: (here[0] ^ z, 0)
                )
                for part in splits
            ],
        ),
        compiler_params=pltpu.CompilerParams(vmem_limit_bytes=VMEM_BYTES),
        cost_estimate=pl.CostEstimate(
            flops=0, bytes_accessed=8 * pieces * rows * width, transcendentals=0
        ),
        name="place",
    )(here, own.reshape(shape), other.reshape(shape))


def gather_group(shard, steps):
    held = with_layout_constraint(shard[None], Layout((0, 1, 2)))
    for axis, bit in steps:
        held = jnp.concatenate([held, swapped(held, axis, bit)], 0)
    return held, swapped(held, "clip", 0)


def reduce_group(pairs, reverse, begun=None):
    clip_count = lax.axis_size("clip")
    uppers = clip_count // 2
    sizes = {"coarse": lax.axis_size("coarse"), "fine": lax.axis_size("fine")}
    me = lax.axis_index("clip")
    width = pairs[0][0].shape[1] // clip_count
    parts = []
    for left, right in pairs:

        def blocks(core):
            return [
                lax.dynamic_slice_in_dim(left, (me ^ (2 * upper + core)) * width, width, 1)
                for upper in range(uppers)
            ]

        away = weight_grad(right, jnp.concatenate(blocks(1), 1)).astype(bf16)
        arrived = swapped(away, "clip", 0)
        kept = weight_grad(right, jnp.concatenate(blocks(0), 1)) + arrived.astype(f32)
        per_block = right.shape[1] // (sizes["coarse"] * sizes["fine"])
        parts.append(
            kept.astype(bf16).reshape(
                sizes["coarse"], sizes["fine"], per_block, uppers * width
            )
        )
    held = parts[0] if len(parts) == 1 else jnp.concatenate(parts, 2)
    if begun is not None:
        begun.append(held)
    coarse = [("coarse", b) for b in range(log2(sizes["coarse"]))][::-1]
    fine = [("fine", b) for b in range(log2(sizes["fine"]))][::-1]
    upper = [("clip", b) for b in range(1, log2(clip_count))][::-1]
    steps = (fine + upper if reverse else upper + fine) + coarse
    for count, (axis, bit) in enumerate(steps):
        if axis == "clip":
            half = held.shape[3] // 2
            away, kept = held[..., half:], held[..., :half]
        else:
            dim = 0 if axis == "coarse" else 1
            split = held.shape[:dim] + (2, held.shape[dim] // 2) + held.shape[dim + 1 :]
            mine = (lax.axis_index(axis) >> bit) & 1
            both = held.reshape(split)
            away = lax.dynamic_index_in_dim(both, 1 - mine, dim, keepdims=False)
            kept = lax.dynamic_index_in_dim(both, mine, dim, keepdims=False)
        total = kept.astype(f32) + swapped(away, axis, bit).astype(f32)
        held = total if count == len(steps) - 1 else total.astype(bf16)
    return held.reshape(held.shape[2], held.shape[3])


def summed_everywhere(values):
    for axis in ("coarse", "clip", "fine"):
        for bit in range(log2(lax.axis_size(axis))):
            values = values + swapped(values, axis, bit)
    return values


def packed(parts):
    flat = jnp.concatenate([part.reshape(-1) for part in parts])
    rows = -(-flat.shape[0] // 8192) * 8
    return jnp.pad(flat, (0, rows * D - flat.shape[0])).reshape(rows, D)


def unpacked(rows, parts):
    flat = rows.reshape(-1)
    out, start = [], 0
    for part in parts:
        out.append(flat[start : start + part.size].reshape(part.shape))
        start += part.size
    return out


def head_rows(ref, start, width):
    return ref[:, 0, :, start : start + width].reshape(-1, width)


def attend_kernel(lengths, x_ref, table_ref, out_ref, probs_ref):
    blocks, unused, block, wide = x_ref.shape
    length = blocks * block
    width = wide // 3
    valid = lengths[pl.program_id(0)]
    table = table_ref[...]
    key_at = lax.broadcasted_iota(jnp.int32, (1, length), 1)
    masked = key_at >= valid
    row_at = lax.broadcasted_iota(jnp.int32, (block, 3 * block), 0)
    offset = lax.broadcasted_iota(jnp.int32, (block, 3 * block), 1) - block - row_at
    for head in range(width // HEAD_SIZE):
        at = head * HEAD_SIZE
        keys = head_rows(x_ref, width + at, HEAD_SIZE)
        values = head_rows(x_ref, 2 * width + at, HEAD_SIZE)
        for part in range(blocks):
            queries = x_ref[part, 0, :, at : at + HEAD_SIZE]
            relative = product_t(queries, table).astype(bf16).astype(f32)
            back = relative[:, :1]
            fore = relative[:, OFFSETS - 1 : OFFSETS]
            band = jnp.concatenate([relative, jnp.zeros((block, 2 * block), f32)], 1)
            band = pltpu.roll(band, block - BACK_REACH, 1, stride=1, stride_axis=0)
            band = jnp.where(offset <= -BACK_REACH, back, jnp.where(offset >= FORE_REACH, fore, band))
            bias = []
            if part > 1:
                bias.append(jnp.broadcast_to(back, (block, (part - 1) * block)))
            bias.append(
                band[:, (block if part == 0 else 0) : (2 * block if part == blocks - 1 else 3 * block)]
            )
            if part < blocks - 2:
                bias.append(jnp.broadcast_to(fore, (block, (blocks - 2 - part) * block)))
            scores = (product_t(queries, keys) + jnp.concatenate(bias, 1)) * HEAD_SIZE ** (-0.5)
            scores = jnp.where(masked, negative_fill, scores)
            shifted = jnp.exp(scores - jnp.max(scores, -1, keepdims=True))
            probs = (shifted * (1.0 / jnp.sum(shifted, -1, keepdims=True))).astype(bf16)
            probs_ref[0, head, part * block : (part + 1) * block, :] = probs
            out_ref[part, 0, :, at : at + HEAD_SIZE] = product(probs, values).astype(bf16)


def attend_back_kernel(x_ref, grad_ref, probs_ref, table_ref, out_ref, table_out, score_g, relative_g):
    blocks, unused, block, wide = x_ref.shape
    width = wide // 3
    table = table_ref[...]
    scale = HEAD_SIZE ** (-0.5)
    row_at = lax.broadcasted_iota(jnp.int32, (block, 3 * block), 0)
    offset = lax.broadcasted_iota(jnp.int32, (block, 3 * block), 1) - block - row_at
    row_two = lax.broadcasted_iota(jnp.int32, (block, 2 * block), 0)
    lane = lax.broadcasted_iota(jnp.int32, (block, TABLE_ROWS), 1)
    zeros = jnp.zeros((block, block), f32)
    table_total = jnp.zeros(table_out.shape[1:], f32)
    for head in range(width // HEAD_SIZE):
        at = head * HEAD_SIZE
        all_queries = head_rows(x_ref, at, HEAD_SIZE)
        keys = head_rows(x_ref, width + at, HEAD_SIZE)
        values = head_rows(x_ref, 2 * width + at, HEAD_SIZE)
        all_grads = head_rows(grad_ref, at, HEAD_SIZE)
        for part in range(blocks):
            rows = slice(part * block, (part + 1) * block)
            grads = grad_ref[part, 0, :, at : at + HEAD_SIZE]
            probs = probs_ref[0, head, rows, :].astype(f32)
            probs_g = product_t(grads, values)
            inner = jnp.sum(probs * probs_g, -1, keepdims=True)
            low = (probs * (probs_g - inner)).astype(bf16)
            score_g[rows, :] = low
            wide_low = low.astype(f32)
            first = (part - 1) * block
            pieces = []
            if part == 0:
                pieces.append(zeros)
            pieces.append(wide_low[:, max(first, 0) : first + 3 * block])
            if part == blocks - 1:
                pieces.append(zeros)
            window = jnp.concatenate(pieces, 1)
            back = jnp.sum(jnp.where(offset <= -BACK_REACH, window, 0.0), -1, keepdims=True)
            fore = jnp.sum(jnp.where(offset >= FORE_REACH, window, 0.0), -1, keepdims=True)
            if part > 1:
                back = back + jnp.sum(wide_low[:, :first], -1, keepdims=True)
            if part < blocks - 2:
                fore = fore + jnp.sum(wide_low[:, first + 3 * block :], -1, keepdims=True)
            band = pltpu.roll(window, 3 * block - (block - BACK_REACH), 1)[:, : 2 * block]
            for bit in range(log2(block)):
                rolled = pltpu.roll(band, 2 * block - (1 << bit), 1)
                band = jnp.where(((row_two >> bit) & 1) == 1, rolled, band)
            band = band[:, :TABLE_ROWS]
            band = jnp.where(lane == 0, back, jnp.where(lane == OFFSETS - 1, fore, band))
            band = jnp.where(lane < OFFSETS, band, 0.0)
            relative = (band * scale).astype(bf16)
            relative_g[rows, :] = relative
            query_g = product(low, keys) * scale + product(relative, table)
            out_ref[part, 0, :, at : at + HEAD_SIZE] = query_g.astype(bf16)
        key_g = (weight_grad(score_g[...], all_queries) * scale).astype(bf16)
        value_g = weight_grad(probs_ref[0, head], all_grads).astype(bf16)
        table_total = table_total + weight_grad(relative_g[...], all_queries)
        for part in range(blocks):
            rows = slice(part * block, (part + 1) * block)
            out_ref[part, 0, :, width + at : width + at + HEAD_SIZE] = key_g[rows]
            out_ref[part, 0, :, 2 * width + at : 2 * width + at + HEAD_SIZE] = value_g[rows]
    table_out[0] = table_total


def attend(x, lengths, table):
    blocks, clips, block, wide = x.shape
    length, heads = blocks * block, wide // 3 // HEAD_SIZE
    return pl.pallas_call(
        attend_kernel,
        out_shape=[
            jax.ShapeDtypeStruct((blocks, clips, block, wide // 3), bf16),
            jax.ShapeDtypeStruct((clips, heads, length, length), bf16),
        ],
        grid_spec=pltpu.PrefetchScalarGridSpec(
            num_scalar_prefetch=1,
            grid=(clips,),
            in_specs=[
                pl.BlockSpec((blocks, 1, block, wide), lambda c, lengths: (0, c, 0, 0)),
                pl.BlockSpec((TABLE_ROWS, HEAD_SIZE), lambda c, lengths: (0, 0)),
            ],
            out_specs=[
                pl.BlockSpec((blocks, 1, block, wide // 3), lambda c, lengths: (0, c, 0, 0)),
                pl.BlockSpec((1, heads, length, length), lambda c, lengths: (c, 0, 0, 0)),
            ],
        ),
        compiler_params=pltpu.CompilerParams(vmem_limit_bytes=VMEM_BYTES),
        cost_estimate=pl.CostEstimate(
            flops=16 * clips * heads * length * length * HEAD_SIZE,
            bytes_accessed=2 * clips * heads * length * length,
            transcendentals=clips * heads * length * length,
        ),
        name="attend",
    )(lengths, x, table)


def attend_back(x, grads, probs, table):
    blocks, clips, block, wide = x.shape
    length, heads = blocks * block, wide // 3 // HEAD_SIZE
    return pl.pallas_call(
        attend_back_kernel,
        out_shape=[
            jax.ShapeDtypeStruct(x.shape, bf16),
            jax.ShapeDtypeStruct((clips, TABLE_ROWS, HEAD_SIZE), f32),
        ],
        grid=(clips,),
        in_specs=[
            pl.BlockSpec((blocks, 1, block, wide), lambda c: (0, c, 0, 0)),
            pl.BlockSpec((blocks, 1, block, wide // 3), lambda c: (0, c, 0, 0)),
            pl.BlockSpec((1, heads, length, length), lambda c: (c, 0, 0, 0)),
            pl.BlockSpec((TABLE_ROWS, HEAD_SIZE), lambda c: (0, 0)),
        ],
        out_specs=[
            pl.BlockSpec((blocks, 1, block, wide), lambda c: (0, c, 0, 0)),
            pl.BlockSpec((1, TABLE_ROWS, HEAD_SIZE), lambda c: (c, 0, 0)),
        ],
        scratch_shapes=[
            pltpu.VMEM((length, length), bf16),
            pltpu.VMEM((length, TABLE_ROWS), bf16),
        ],
        compiler_params=pltpu.CompilerParams(vmem_limit_bytes=VMEM_BYTES),
        cost_estimate=pl.CostEstimate(
            flops=32 * clips * heads * length * length * HEAD_SIZE,
            bytes_accessed=2 * clips * heads * length * length,
            transcendentals=0,
        ),
        name="attend_back",
    )(x, grads, probs, table)


def exchanged(rows):
    return lax.all_to_all(rows, SEQ, 0, 0, tiled=True)


class HeadsSplit:
    def __init__(self, clips, frames, lengths, table_low):
        self.clips, self.frames, self.lengths = clips, frames, lengths
        self.peers = lax.axis_size(SEQ)
        self.table = jnp.pad(table_low, ((0, TABLE_ROWS - OFFSETS), (0, 0)))

    def to_heads(self, rows):
        wide = rows.shape[1] // self.peers
        split = rows.reshape(self.clips * self.frames, self.peers, wide).transpose(1, 0, 2)
        return exchanged(split.reshape(self.peers, self.clips, self.frames, wide))

    def to_rows(self, blocks):
        wide = blocks.shape[3]
        back = exchanged(blocks).reshape(self.peers, self.clips * self.frames, wide)
        return back.transpose(1, 0, 2).reshape(self.clips * self.frames, self.peers * wide)

    def forward(self, rows):
        self.x = self.to_heads(rows)
        mixed, self.probs = attend(self.x, self.lengths, self.table)
        return self.to_rows(mixed)

    def backward(self, mixed_grad):
        grads, table_g = attend_back(self.x, self.to_heads(mixed_grad), self.probs, self.table)
        return self.to_rows(grads), jnp.sum(table_g, 0)[:OFFSETS]


class KeysGathered:
    def __init__(self, clips, frames, lengths, table_low):
        self.clips, self.frames, self.table = clips, frames, table_low
        self.peers = lax.axis_size(SEQ)
        length = frames * self.peers
        query_pos = lax.axis_index(SEQ) * frames + jnp.arange(frames, dtype=jnp.int32)
        key_pos = jnp.arange(length, dtype=jnp.int32)
        offset = jnp.clip(key_pos[None, :] - query_pos[:, None], -BACK_REACH, FORE_REACH)
        self.onehot = (
            (offset + BACK_REACH)[None] == jnp.arange(OFFSETS, dtype=jnp.int32)[:, None, None]
        ).astype(bf16)
        self.key_valid = key_pos[None, :] < lengths[:, None]

    def heads(self, rows):
        return rows.reshape(rows.shape[0], rows.shape[1], HEADS, HEAD_SIZE)

    def scores(self):
        dotted = jnp.einsum("cihd,cjhd->chij", self.queries, self.keys, preferred_element_type=f32)
        bias = jnp.einsum("chir,rij->chij", self.relative, self.onehot, preferred_element_type=f32)
        scaled = (dotted + bias) * HEAD_SIZE ** (-0.5)
        return jnp.where(self.key_valid[:, None, None, :], scaled, negative_fill)

    def forward(self, rows):
        split = rows.reshape(self.clips, self.frames, self.peers, 3, -1)
        flat = [split[:, :, :, which].reshape(self.clips, self.frames, D) for which in range(3)]
        self.queries = self.heads(flat[0])
        self.keys = self.heads(lax.all_gather(flat[1], SEQ, axis=1, tiled=True))
        self.values = self.heads(lax.all_gather(flat[2], SEQ, axis=1, tiled=True))
        self.relative = jnp.einsum(
            "cihd,rd->chir", self.queries, self.table, preferred_element_type=f32
        ).astype(bf16)
        scores = self.scores()
        top = jnp.max(scores, -1, keepdims=True)
        self.log_total = jnp.log(jnp.sum(jnp.exp(scores - top), -1, keepdims=True)) + top
        probs = jnp.exp(scores - self.log_total).astype(bf16)
        mixed = jnp.einsum("chij,cjhd->cihd", probs, self.values, preferred_element_type=f32)
        return mixed.astype(bf16).reshape(self.clips * self.frames, D)

    def backward(self, mixed_grad):
        scale = HEAD_SIZE ** (-0.5)
        grads = self.heads(mixed_grad.reshape(self.clips, self.frames, D))
        probs = jnp.exp(self.scores() - self.log_total)
        probs_g = jnp.einsum("cihd,cjhd->chij", grads, self.values, preferred_element_type=f32)
        inner = jnp.sum(probs * probs_g, -1, keepdims=True)
        scores_g = (probs * (probs_g - inner)).astype(bf16)
        relative_g = (
            jnp.einsum("chij,rij->chir", scores_g, self.onehot, preferred_element_type=f32) * scale
        ).astype(bf16)
        query_g = jnp.einsum(
            "chij,cjhd->cihd", scores_g, self.keys, preferred_element_type=f32
        ) * scale + jnp.einsum("chir,rd->cihd", relative_g, self.table, preferred_element_type=f32)
        table_g = jnp.einsum(
            "chir,cihd->rd", relative_g, self.queries, preferred_element_type=f32
        )
        key_g = (
            jnp.einsum("chij,cihd->cjhd", scores_g, self.queries, preferred_element_type=f32) * scale
        )
        value_g = jnp.einsum(
            "chij,cihd->cjhd", probs.astype(bf16), grads, preferred_element_type=f32
        )
        length = self.frames * self.peers
        both = [
            lax.psum_scatter(
                terms.reshape(self.clips, length, D).astype(bf16),
                SEQ,
                scatter_dimension=1,
                tiled=True,
            )
            for terms in (key_g, value_g)
        ]
        rows = self.clips * self.frames
        parts = [query_g.astype(bf16)] + both
        joined = jnp.stack([part.reshape(rows, self.peers, -1) for part in parts], 2)
        return joined.reshape(rows, 3 * D), table_g


def feed_forward(hidden, scale, shift, w_in, b_in, w_out, b_out):
    normed = layer_norm(hidden, scale, shift).astype(bf16)
    upper = product_t(normed, w_in) + b_in
    acted = jax.nn.silu(upper).astype(bf16)
    return (product_t(acted, w_out) + b_out, (normed, upper, acted))


def feed_back(grad, hidden, scale, shift, w_in, w_out, saved):
    normed, upper, acted = saved
    grad_low = grad.astype(bf16)
    unused, silu_pull = jax.vjp(jax.nn.silu, upper)
    upper_grad = silu_pull(product(grad_low, w_out))[0].astype(bf16)
    hidden_grad, scale_grad, shift_grad = norm_back(
        hidden, scale, shift, product(upper_grad, w_in)
    )
    return (
        hidden_grad,
        (normed, upper_grad),
        (acted, grad_low),
        scale_grad,
        shift_grad,
        column_sum(upper_grad),
        column_sum(grad_low),
    )


def per_device(
    frames_in,
    clip_lengths,
    out_grad,
    first_up,
    first_down,
    query_weight,
    key_weight,
    value_weight,
    output_weight,
    pointwise_in,
    pointwise_out,
    second_up,
    second_down,
    norm_scales,
    norm_shifts,
    hidden_biases,
    width_biases,
    value_bias,
    relative_table,
    depth_kernel,
):
    clips, frames, unused = frames_in.shape
    rows = clips * frames
    peers = lax.axis_size(SEQ)

    orders = [gather_steps(False), gather_steps(True)]
    groups = (
        ([first_up],),
        ([first_down],),
        ([query_weight, key_weight, value_weight], [output_weight]),
        ([pointwise_in], [pointwise_out]),
        ([second_up],),
        ([second_down],),
    )
    placed = []
    for number, group in enumerate(groups):
        shards = [shard.astype(bf16).T for part in group for shard in part]
        splits = tuple(sum(shard.shape[1] for shard in part) for part in group)
        order = number % 2
        own, other = gather_group(jnp.concatenate(shards, 0), orders[order])
        placed.extend(place_whole(own, other, order == 1, splits))
    (
        up_first,
        down_first,
        inputs_full,
        output_full,
        inner_full,
        outer_full,
        up_second,
        down_second,
    ) = placed

    base = lax.axis_index(SEQ) * frames
    table_low = relative_table.astype(bf16)
    query_pos = base + jnp.arange(frames, dtype=jnp.int32)
    frame_valid = (query_pos[None, :] < clip_lengths[:, None]).reshape(rows, 1)
    share = D // peers
    inputs_bias = jnp.stack(
        [
            width_biases[1].reshape(peers, share),
            jnp.zeros((peers, share), f32),
            value_bias.reshape(peers, share),
        ],
        1,
    ).reshape(3 * D)

    start_rows = frames_in.astype(f32).reshape(rows, D)
    branch_one, first_saved = feed_forward(
        start_rows,
        norm_scales[0],
        norm_shifts[0],
        up_first,
        hidden_biases[0],
        down_first,
        width_biases[0],
    )
    after_first = start_rows + 0.5 * branch_one
    att_normed = layer_norm(after_first, norm_scales[1], norm_shifts[1]).astype(bf16)
    attention_rows = (product_t(att_normed, inputs_full) + inputs_bias).astype(bf16)
    split_heads = HEADS % peers == 0 and (D // peers) % 128 == 0
    attention = (HeadsSplit if split_heads else KeysGathered)(
        clips, frames, clip_lengths, table_low
    )
    mixed = attention.forward(attention_rows)
    after_attention = after_first + product_t(mixed, output_full) + width_biases[2]
    conv_normed = jnp.where(
        frame_valid, layer_norm(after_attention, norm_scales[2], norm_shifts[2]), 0.0
    ).astype(bf16)
    doubled = product_t(conv_normed, inner_full)
    gated = glu_gate(doubled).astype(bf16).reshape(clips, frames, D)
    carried = passed_along(gated[:, frames - KERNEL + 1 :], SEQ, 1)
    extended = jnp.concatenate([carried, gated], 1).astype(f32)
    mixed_conv = depthwise(extended, depth_kernel).reshape(rows, D)
    conv_acted = post_norm(mixed_conv, norm_scales[3], norm_shifts[3]).astype(bf16)
    after_conv = after_attention + product_t(conv_acted, outer_full)
    branch_two, second_saved = feed_forward(
        after_conv,
        norm_scales[4],
        norm_shifts[4],
        up_second,
        hidden_biases[1],
        down_second,
        width_biases[3],
    )
    after_second = after_conv + 0.5 * branch_two
    layer_out = (
        layer_norm(after_second, norm_scales[5], norm_shifts[5])
        .astype(bf16)
        .reshape(clips, frames, D)
    )

    final_grad, final_scale, final_shift = norm_back(
        after_second, norm_scales[5], norm_shifts[5], out_grad.astype(f32).reshape(rows, D)
    )
    (
        second_in,
        second_up_pair,
        second_down_pair,
        second_scale,
        second_shift,
        second_hidden,
        second_width,
    ) = feed_back(
        0.5 * final_grad,
        after_conv,
        norm_scales[4],
        norm_shifts[4],
        up_second,
        down_second,
        second_saved,
    )
    second_down_g = reduce_group([second_down_pair], False)
    second_up_g = reduce_group([second_up_pair], True)
    grad_conv = final_grad + second_in
    conv_low = grad_conv.astype(bf16)
    unused, post_pull = jax.vjp(post_norm, mixed_conv, norm_scales[3], norm_shifts[3])
    mixed_g, depth_scale, depth_shift = post_pull(product(conv_low, outer_full))
    unused, depth_pull = jax.vjp(depthwise, extended, depth_kernel)
    extended_g, kernel_g = depth_pull(mixed_g.reshape(clips, frames, D))
    returned = passed_along(extended_g[:, : KERNEL - 1].astype(bf16), SEQ, -1).astype(f32)
    own_g = extended_g[:, KERNEL - 1 :]
    gated_g = jnp.concatenate(
        [own_g[:, : frames - KERNEL + 1], own_g[:, frames - KERNEL + 1 :] + returned], 1
    ).reshape(rows, D)
    unused, glu_pull = jax.vjp(glu_gate, doubled)
    doubled_g = glu_pull(gated_g)[0].astype(bf16)
    normed_g = jnp.where(frame_valid, product(doubled_g, inner_full), 0.0)
    conv_in_g, conv_scale, conv_shift = norm_back(
        after_attention, norm_scales[2], norm_shifts[2], normed_g
    )
    grad_att = grad_conv + conv_in_g
    att_low = grad_att.astype(bf16)
    middle_g = reduce_group(
        [(conv_normed, doubled_g), (conv_acted, conv_low), (mixed, att_low)], False
    )
    mixed_grad = product(att_low, output_full).astype(bf16)
    attention_g, table_g = attention.backward(mixed_grad)
    begun = []
    inputs_g = reduce_group([(att_normed, attention_g)], False, begun)
    att_in_g, att_scale, att_shift = norm_back(
        after_first, norm_scales[1], norm_shifts[1], product(attention_g, inputs_full)
    )
    grad_first = grad_att + att_in_g
    (
        first_in,
        first_up_pair,
        first_down_pair,
        first_scale,
        first_shift,
        first_hidden,
        first_width,
    ) = feed_back(
        0.5 * grad_first,
        start_rows,
        norm_scales[0],
        norm_shifts[0],
        up_first,
        down_first,
        first_saved,
    )
    first_down_g = reduce_group([first_down_pair], False, begun)
    first_up_g = reduce_group([first_up_pair], True, begun)
    in_grad = (grad_first + first_in).astype(bf16).reshape(clips, frames, D)

    attention_sums = column_sum(attention_g).reshape(peers, 3, share)
    small = [
        jnp.stack([first_scale, att_scale, conv_scale, depth_scale, second_scale, final_scale]),
        jnp.stack([first_shift, att_shift, conv_shift, depth_shift, second_shift, final_shift]),
        jnp.stack([first_hidden, second_hidden]),
        jnp.stack(
            [first_width, attention_sums[:, 0].reshape(D), column_sum(att_low), second_width]
        ),
        attention_sums[:, 2].reshape(D),
        table_g,
        kernel_g,
    ]
    values, unused = lax.optimization_barrier((packed(small), begun))
    small = unpacked(summed_everywhere(values), small)

    inner_n = 2 * D // peers
    outer_n = D // peers
    return (
        layer_out,
        in_grad,
        first_up_g.T,
        first_down_g.T,
        inputs_g[:share].T,
        inputs_g[share : 2 * share].T,
        inputs_g[2 * share :].T,
        middle_g[inner_n + outer_n :].T,
        middle_g[:inner_n].T,
        middle_g[inner_n : inner_n + outer_n].T,
        second_up_g.T,
        second_down_g.T,
        *small,
    )


def solution(mesh):
    block = P("clip", ("coarse", "fine"))
    rows = P("clip", ("coarse", "fine"), None)
    in_specs = (rows, P("clip"), rows) + (block,) * 10 + (P(),) * 7
    out_specs = (rows, rows) + (block,) * 10 + (P(),) * 7
    return jax.shard_map(
        per_device, mesh=mesh, in_specs=in_specs, out_specs=out_specs, check_vma=False
    )
```
